32 devices in a mesh: groups: 2 (over x), tensor: 16 (over z, y, core).
Axes of the slice: x: 2, y: 2, z: 4, core: 2. Of those that a mesh axis runs over, the one named last changes fastest.
Arguments:
- tokens: bfloat16 [256, 8192], P(('groups', 'tensor')), parts along dimension 0, may hold values from -6 to 6
- gate_weight: bfloat16 [8192, 28672], P(None, 'tensor'), may hold values from -0.0625 to 0.0625
- up_weight: bfloat16 [8192, 28672], P(None, 'tensor'), may hold values from -0.0625 to 0.0625
- adapter_down_weight: bfloat16 [32, 8192, 64], P(('groups', 'tensor')), parts along dimension 0, may hold values from -0.0625 to 0.0625
- adapter_up_weight: bfloat16 [32, 64, 28672], P('groups', None, 'tensor'), parts along dimension 0, may hold values from -0.75 to 0.75
- request_adapter_index: int32 [256], P('groups'), parts along dimension 0, may hold values from 0 to 15, as said below
- adapter_request_lists: int32 [32, 32], P('groups'), parts along dimension 0, may hold values from 0 to 128, as said below
- placement: int32 [32], P('groups'), parts along dimension 0, may hold values from 0 to 15, each once
Outputs:
- hidden: bfloat16 [256, 28672], P('groups', 'tensor'), parts along dimension 0
The draws below stay inside these ranges and needn't reach their ends.
There are 2 independent parts, one for each index of `groups`. The reference program is written for one: setup_inputs(seed, part) draws one part's arguments, and reference() takes and returns one part's arrays. A program takes and returns all parts, laid end to end along the dimension named above; an argument that names none is the same for every part. Nothing has to cross between parts.
Inputs may be any that keep to these rules, and one draw needn't show every extreme that they name: Each request r appears exactly once in adapter_request_lists, in the row request_adapter_index[r]; the other entries equal 128. `request_adapter_index`: at most 32 requests share one adapter; some adapter has exactly 32.
All inputs are finite; a program needn't handle non-finite values.
Results may differ from the reference program's by a relative error of at most 0.0041.
Values may be sent and summed in bfloat16 or wider, within the bound.
No kernel may reach another device: no remote copies, remote signals or barrier semaphores. Data moves between devices by JAX's collectives and lax.ppermute only.
A program may use at most 192 MiB of HBM per device.

```python
import jax
import jax.numpy as jnp
from jax import lax

MODEL_WIDTH = 8192
HIDDEN_UNITS = 28672
ADAPTER_RANK = 64
CAP = 32
REQUESTS = 128
ADAPTER_COUNT = 16


def assign_slots(base_key):
    keys = jax.random.split(base_key, 4)
    slot_count = ADAPTER_COUNT * CAP
    levels = jax.random.randint(keys[0], (ADAPTER_COUNT,), 0, 8)
    hottest = jax.random.randint(keys[1], (), 0, ADAPTER_COUNT)
    noise = jax.random.randint(keys[2], (ADAPTER_COUNT, CAP), 0, 256)
    position = jnp.arange(CAP, dtype=jnp.int32)
    scores = noise + levels[:, None] * 64 - position[None, :] * 48
    owners = jnp.arange(ADAPTER_COUNT, dtype=jnp.int32)[:, None] + jnp.zeros((1, CAP), jnp.int32)
    scores = jnp.where(owners == hottest, 1 << 20, scores)
    ordering = jnp.argsort(-scores.reshape(-1), stable=True)
    chosen = ordering[:REQUESTS].astype(jnp.int32)
    shuffled = jax.random.permutation(keys[3], REQUESTS).astype(jnp.int32)
    ids = jnp.zeros((REQUESTS,), jnp.int32).at[shuffled].set(chosen // CAP)
    lists = jnp.full((slot_count,), REQUESTS, jnp.int32).at[chosen].set(shuffled)
    return (ids, lists.reshape(ADAPTER_COUNT, CAP))


def draw_request_adapter_index(key, part):
    ids, lists = assign_slots(key)
    return ids


def draw_adapter_request_lists(key, part):
    ids, lists = assign_slots(key)
    return lists


def steps_of(key, dims, shards, low, largest):
    loudness, own = 1.0, jax.random.fold_in(key, 6)
    for dim, blocks in shards:
        draws = jnp.exp(jax.random.uniform(jax.random.fold_in(own, dim), (blocks,), jnp.float32, low / len(shards), largest / len(shards)))
        loudness = loudness * jnp.repeat(draws, dims[dim] // blocks).reshape([-1 if axis == dim else 1 for axis in range(len(dims))])
    return loudness


def gaussian(stream_key, extent, scale, reach, shards=(), kind=jnp.bfloat16):
    result = scale * jax.random.normal(stream_key, extent, jnp.float32)
    if shards:
        result = result * steps_of(stream_key, extent, shards, -0.22, 0.18)
    return jnp.clip(result, -reach, reach).astype(kind)


def setup_inputs(seed: int = 0, part: int = 0) -> dict:
    key_of = jax.random.split(jax.random.key(seed), 9)
    part_keys = jax.random.split(jax.random.fold_in(key_of[8], part), 9)
    tokens = gaussian(part_keys[0], (REQUESTS, MODEL_WIDTH), 1.0, 6.0, ((0, 16),))
    gate_weight = gaussian(key_of[1], (MODEL_WIDTH, HIDDEN_UNITS), MODEL_WIDTH ** -0.5, 0.0625, ((1, 16),))
    up_weight = gaussian(key_of[2], (MODEL_WIDTH, HIDDEN_UNITS), MODEL_WIDTH ** -0.5, 0.0625, ((1, 16),))
    adapter_down_weight = gaussian(part_keys[3], (ADAPTER_COUNT, MODEL_WIDTH, ADAPTER_RANK), MODEL_WIDTH ** -0.5, 0.0625, ((0, 16),))
    adapter_up_weight = gaussian(part_keys[4], (ADAPTER_COUNT, ADAPTER_RANK, HIDDEN_UNITS), ADAPTER_RANK ** -0.5, 0.75, ((2, 16),))
    request_adapter_index = draw_request_adapter_index(jax.random.fold_in(jax.random.fold_in(key_of[8], part), 71), part)
    adapter_request_lists = draw_adapter_request_lists(jax.random.fold_in(jax.random.fold_in(key_of[8], part), 71), part)
    placement = jax.random.permutation(part_keys[7], ADAPTER_COUNT).astype(jnp.int32)
    return dict(tokens=tokens, gate_weight=gate_weight, up_weight=up_weight, adapter_down_weight=adapter_down_weight, adapter_up_weight=adapter_up_weight, request_adapter_index=request_adapter_index, adapter_request_lists=adapter_request_lists, placement=placement)


def reference(tokens, gate_weight, up_weight, adapter_down_weight, adapter_up_weight, request_adapter_index, adapter_request_lists, placement):
    request_batch = tokens.shape[0]
    gate_pre = jnp.dot(tokens, gate_weight, preferred_element_type=jnp.float32)
    up_pre = jnp.dot(tokens, up_weight, preferred_element_type=jnp.float32)

    def adapter_rows(inputs):
        row_list, adapter_store_slot = inputs
        valid = row_list < request_batch
        input_rows = jnp.take(tokens, jnp.minimum(row_list, request_batch - 1).astype(jnp.int32), axis=0)
        input_rows = jnp.where(valid[:, None], input_rows, jnp.zeros_like(input_rows))
        return jnp.dot(input_rows, adapter_down_weight[adapter_store_slot], preferred_element_type=jnp.float32)

    low_rank_output = lax.map(adapter_rows, (adapter_request_lists, placement))
    partial_value = jnp.zeros((request_batch, ADAPTER_RANK), jnp.float32).at[adapter_request_lists.reshape(-1)].add(
        low_rank_output.reshape(-1, ADAPTER_RANK), mode="drop")
    mixed = partial_value.astype(jnp.bfloat16)

    def row_delta(inputs):
        row_low_rank, adapter_index = inputs
        return jnp.dot(row_low_rank[None, :], adapter_up_weight[adapter_index], preferred_element_type=jnp.float32)[0]

    delta = lax.map(row_delta, (mixed, request_adapter_index))
    return (jax.nn.silu(gate_pre) * (up_pre + delta)).astype(jnp.bfloat16)
```

```python
import jax
import jax.numpy as jnp
from jax import lax
from jax.sharding import PartitionSpec as P


def plan(count):
    lines = 1
    while lines * lines < count // 2:
        lines *= 2
    return lines, count // 2 // lines


def body(
    tokens,
    gate_weight,
    up_weight,
    adapter_down_weight,
    adapter_up_weight,
    request_adapter_index,
    adapter_request_lists,
    placement,
):
    count = lax.axis_size("tensor")
    depth, width = plan(count)
    rows = tokens.shape[0]
    requests = request_adapter_index.shape[0]
    adapters = placement.shape[0]
    rank_width = adapter_down_weight.shape[2]
    own = lax.axis_index("tensor")

    def send(value, da, db, dc):
        pairs = []
        for i in range(count):
            a, b, c = i // (2 * width), i // 2 % width, i % 2
            pairs.append((i, ((a + da) % depth * width + (b + db) % width) * 2 + (c + dc) % 2))
        return lax.ppermute(value, "tensor", pairs)

    by_line = [tokens] + [send(tokens, j, 0, 0) for j in range(1, depth)]
    plane = list(by_line)
    for k in range(1, width):
        plane += [send(block, 0, k, 0) for block in by_line]
    half = jnp.concatenate(plane, 0)
    other = send(half, 0, 0, 1)
    gathered = jnp.concatenate([half, other], 0)

    slot = jnp.arange(requests, dtype=jnp.int32)
    block, inner = slot // rows, slot % rows
    j, k, m = block % depth, block // depth % width, block // (depth * width)
    origin = ((own // (2 * width) - j) % depth * width + (own // 2 - k) % width) * 2 + (own + m) % 2
    row_id = origin * rows + inner

    owner = jnp.sum(jnp.where(placement == own, jnp.arange(adapters, dtype=jnp.int32), 0))
    wanted = lax.dynamic_slice_in_dim(adapter_request_lists, owner, 1, 0)[0]
    picker = (wanted[:, None] == row_id[None, :]).astype(jnp.bfloat16)
    picked = jnp.dot(picker, gathered, preferred_element_type=jnp.float32).astype(jnp.bfloat16)
    low_rank = jnp.dot(picked, adapter_down_weight[0], preferred_element_type=jnp.float32)
    spread = (jnp.arange(requests, dtype=jnp.int32)[:, None] == wanted[None, :]).astype(jnp.bfloat16)
    mixed = jnp.dot(spread, low_rank.astype(jnp.bfloat16), preferred_element_type=jnp.float32)
    mixed = mixed.astype(jnp.bfloat16)
    step = 1
    while step < count:
        mixed = mixed + lax.ppermute(mixed, "tensor", [(i, i ^ step) for i in range(count)])
        step *= 2

    gate_pre = jnp.dot(gathered, gate_weight, preferred_element_type=jnp.float32)
    up_pre = jnp.dot(gathered, up_weight, preferred_element_type=jnp.float32)
    here = (row_id[:, None] == jnp.arange(requests, dtype=jnp.int32)[None, :]).astype(jnp.bfloat16)
    mine = jnp.dot(here, mixed, preferred_element_type=jnp.float32).astype(jnp.bfloat16)
    index = jnp.take(request_adapter_index, row_id)
    chosen = index[:, None] == jnp.arange(adapters, dtype=jnp.int32)[None, :]
    expanded = jnp.where(chosen[:, :, None], mine[:, None, :], jnp.zeros((), jnp.bfloat16))
    delta = jnp.dot(
        expanded.reshape(requests, adapters * rank_width),
        adapter_up_weight.reshape(adapters * rank_width, -1),
        preferred_element_type=jnp.float32,
    )
    hidden = (jax.nn.silu(gate_pre) * (up_pre + delta)).astype(jnp.bfloat16)
    return jnp.dot(here.T, hidden, preferred_element_type=jnp.float32).astype(jnp.bfloat16)


def solution(mesh):
    in_specs = (
        P(("groups", "tensor"), None),
        P(None, "tensor"),
        P(None, "tensor"),
        P(("groups", "tensor"), None, None),
        P("groups", None, "tensor"),
        P("groups"),
        P("groups", None),
        P("groups"),
    )
    out_specs = P("groups", "tensor")
    return jax.shard_map(body, mesh=mesh, in_specs=in_specs, out_specs=out_specs, check_vma=False)
```

```python
import functools

import jax
import jax.numpy as jnp
from jax import lax
from jax.experimental import pallas as pl
from jax.experimental.pallas import tpu as pltpu
from jax.sharding import PartitionSpec as P

TILE = 256
PIECES = 4
NEAR = pl.BlockSpec(memory_space=pltpu.VMEM)
FAR = pl.BlockSpec(memory_space=pl.ANY)
STORED = pl.BlockSpec(memory_space=pltpu.HBM)


def near(value):
    return pltpu.with_memory_space_constraint(value, pltpu.VMEM)


def far(value):
    return pltpu.with_memory_space_constraint(value, pltpu.HBM)


def plan(count):
    lines = 1
    while lines * lines < count // 2:
        lines *= 2
    return lines, count // 2 // lines


def send(value, da, db, dc):
    count = lax.axis_size("tensor")
    depth, width = plan(count)
    pairs = []
    for i in range(count):
        a, b, c = i // (2 * width), i // 2 % width, i % 2
        pairs.append((i, ((a + da) % depth * width + (b + db) % width) * 2 + (c + dc) % 2))
    return lax.ppermute(value, "tensor", pairs)


def fetch_kernel(start, skipped, source, *refs):
    target, sems = refs[skipped:]
    rows = target.shape[0] // sems.shape[0]
    copies = [
        pltpu.make_async_copy(
            source.at[pl.ds(start + i * rows, rows)], target.at[pl.ds(i * rows, rows)], sems.at[i]
        )
        for i in range(sems.shape[0])
    ]
    for copy in copies:
        copy.start()
    for copy in copies:
        copy.wait()


def fetch(weight, start, rows, name, after=()):
    return pl.pallas_call(
        functools.partial(fetch_kernel, start, len(after)),
        out_shape=pltpu.VMEM((rows, weight.shape[1]), weight.dtype),
        in_specs=[STORED] + [FAR] * len(after),
        out_specs=NEAR,
        scratch_shapes=[pltpu.SemaphoreType.DMA((4,))],
        cost_estimate=pl.CostEstimate(
            flops=0, bytes_accessed=rows * weight.shape[1] * 2, transcendentals=0
        ),
        compiler_params=pltpu.CompilerParams(vmem_limit_bytes=1 << 20),
        name=name,
    )(far(weight), *after)


def across(row):
    n = row.shape[1]
    return jnp.broadcast_to(row, (n, n)).T


def pack_kernel(n, *refs):
    for i in range(n):
        refs[-1][i] = refs[i][...]


def pack(blocks, after):
    rows, model = blocks[0].shape
    n = len(blocks)
    return pl.pallas_call(
        functools.partial(pack_kernel, n),
        out_shape=pltpu.VMEM((n, rows, model), jnp.bfloat16),
        in_specs=[NEAR] * n + [FAR] * len(after),
        out_specs=NEAR,
        cost_estimate=pl.CostEstimate(flops=0, bytes_accessed=1 << 18, transcendentals=0),
        compiler_params=pltpu.CompilerParams(vmem_limit_bytes=1 << 20),
        name="pack",
    )(*[near(v) for v in blocks], *after)


def tie_kernel(*refs):
    pass


def tie(value, after):
    return pl.pallas_call(
        tie_kernel,
        out_shape=jax.ShapeDtypeStruct(value.shape, value.dtype),
        in_specs=[FAR] * (1 + len(after)),
        out_specs=FAR,
        input_output_aliases={0: 0},
        cost_estimate=pl.CostEstimate(flops=0, bytes_accessed=1 << 10, transcendentals=0),
        compiler_params=pltpu.CompilerParams(vmem_limit_bytes=1 << 20),
        name="tie",
    )(value, *after)


def collect_kernel(depth, width, placement, index, down, *refs):
    blocks = 2 * width
    mine, theirs = refs[:blocks], refs[blocks : 2 * blocks]
    packed, low = refs[2 * blocks :]
    own = lax.axis_index("tensor")
    a, b, c = own // (2 * width), own // 2 % width, own % 2
    rows = mine[0].shape[0]
    for k in range(width):
        for j in range(depth):
            chip = lax.rem(a - j + depth, depth) * width + lax.rem(b - k + width, width)
            if j == 0:
                p, q = mine[2 * k][...], theirs[2 * k][...]
            else:
                p, q = mine[2 * k + 1][j - 1], theirs[2 * k + 1][j - 1]
            first, second = jnp.where(c == 0, p, q), jnp.where(c == 0, q, p)
            packed[pl.ds(pl.multiple_of(chip * 2 * rows, 2 * rows), 2 * rows), :] = (
                jnp.concatenate([first, second], 0)
            )
    full = lax.dot_general(
        packed[...], down[...], (((1,), (1,)), ((), ())), preferred_element_type=jnp.float32
    )
    ids = lax.broadcasted_iota(jnp.int32, placement.shape, 1)
    owner = jnp.sum(jnp.where(placement[...] == own, ids, 0), axis=1, keepdims=True)
    chosen = across(jnp.where(index[...] == owner, 1, 0))[:, : full.shape[1]]
    low[...] = jnp.where(chosen == 1, full, 0.0).astype(low.dtype)


def collect(placement, index, down, mine, theirs, depth, width):
    rows, model = mine[0].shape
    requests = 2 * depth * width * rows
    return pl.pallas_call(
        functools.partial(collect_kernel, depth, width),
        out_shape=[
            pltpu.VMEM((requests, model), jnp.bfloat16),
            jax.ShapeDtypeStruct((requests, down.shape[0]), jnp.bfloat16),
        ],
        in_specs=[NEAR] * (3 + 4 * width),
        out_specs=[NEAR] * 2,
        cost_estimate=pl.CostEstimate(
            flops=2 * requests * model * 64, bytes_accessed=1 << 20, transcendentals=0
        ),
        compiler_params=pltpu.CompilerParams(vmem_limit_bytes=4 << 20),
        name="collect",
    )(placement, index, down, *[near(v) for v in mine], *[near(v) for v in theirs])


def add_kernel(*refs):
    total = refs[0][...]
    for ref in refs[1:-1]:
        total = total + ref[...]
    refs[-1][...] = total


def add(*values):
    return pl.pallas_call(
        add_kernel,
        out_shape=jax.ShapeDtypeStruct(values[0].shape, values[0].dtype),
        in_specs=[NEAR] * len(values),
        out_specs=NEAR,
        cost_estimate=pl.CostEstimate(flops=0, bytes_accessed=1 << 14, transcendentals=0),
        compiler_params=pltpu.CompilerParams(vmem_limit_bytes=1 << 20),
        name="add",
    )(*values)


def piecewise(tokens, pieces, start, here):
    total = None
    for piece in pieces:
        rows = piece.shape[0]
        term = jnp.dot(
            tokens[:, start : start + rows], piece[:, here], preferred_element_type=jnp.float32
        )
        total = term if total is None else total + term
        start += rows
    return total


def multiply_kernel(start, n, begun, fetched, *refs):
    tokens, refs = refs[1], refs[2:]
    pieces, refs = refs[:n], refs[n:]
    before, refs = refs[:begun], refs[begun:]
    copies = []
    if fetched:
        source, out, *targets, sems = refs
        first = fetched[0]
        for i, target in enumerate(targets):
            rows = target.shape[0]
            copies.append(
                pltpu.make_async_copy(source.at[pl.ds(first, rows)], target, sems.at[i])
            )
            first += rows
    else:
        (out,) = refs
    for copy in copies:
        copy.start()

    @pl.loop(0, out.shape[1] // TILE)
    def _(i):
        here = pl.ds(pl.multiple_of(i * TILE, TILE), TILE)
        total = piecewise(tokens, pieces, start, here)
        if begun:
            total = total + before[0][:, here]
        out[:, here] = total

    for copy in copies:
        copy.wait()


def multiply(after, tokens, pieces, start, begun, source, fetched, name):
    requests = tokens.shape[0]
    hidden = pieces[0].shape[1]
    out_shape = [pltpu.VMEM((requests, hidden), jnp.float32)]
    operands = [after, near(tokens)] + [near(p) for p in pieces] + [near(b) for b in begun]
    in_specs = [FAR] + [NEAR] * (len(operands) - 1)
    scratch = []
    if fetched:
        operands.append(far(source))
        in_specs.append(STORED)
        out_shape += [pltpu.VMEM((r, hidden), source.dtype) for r in fetched[1:]]
        scratch = [pltpu.SemaphoreType.DMA((len(fetched) - 1,))]
    return pl.pallas_call(
        functools.partial(multiply_kernel, start, len(pieces), len(begun), fetched),
        out_shape=out_shape,
        in_specs=in_specs,
        out_specs=[NEAR] * len(out_shape),
        scratch_shapes=scratch,
        cost_estimate=pl.CostEstimate(
            flops=2 * requests * sum(p.shape[0] for p in pieces) * hidden,
            bytes_accessed=16 << 20,
            transcendentals=0,
        ),
        compiler_params=pltpu.CompilerParams(vmem_limit_bytes=2 << 20),
        name=name,
    )(*operands)


def finish_kernel(start, n, m, index, tokens, adapter_up, gate_pre, up_pre, *refs):
    pieces, refs = refs[:n], refs[n:]
    lows, refs = refs[:m], refs[m:]
    out, near_up, expanded, sem = refs
    rank = lows[0].shape[1]
    copy = pltpu.make_async_copy(adapter_up, near_up, sem)
    copy.start()
    mixed = lows[0][...]
    for low in lows[1:]:
        mixed = mixed + low[...]
    group = TILE // rank
    lane = lax.broadcasted_iota(jnp.int32, (rank, TILE), 1)
    repeat = (lane % rank == lax.broadcasted_iota(jnp.int32, (rank, TILE), 0)).astype(jnp.bfloat16)
    wide = jnp.dot(mixed, repeat, preferred_element_type=jnp.float32)
    of_lane = lax.broadcasted_iota(jnp.int32, (mixed.shape[0], TILE), 1) // rank
    relative = jnp.concatenate([across(index[...])] * (TILE // mixed.shape[0]), 1) - of_lane
    for i in range(expanded.shape[1] // TILE):
        expanded[:, i * TILE : (i + 1) * TILE] = jnp.where(
            relative == i * group, wide, 0.0
        ).astype(jnp.bfloat16)
    copy.wait()

    @pl.loop(0, out.shape[1] // TILE)
    def _(i):
        here = pl.ds(pl.multiple_of(i * TILE, TILE), TILE)
        up = up_pre[:, here] + piecewise(tokens, pieces, start, here)
        up = up + jnp.dot(expanded[...], near_up[:, here], preferred_element_type=jnp.float32)
        gate = gate_pre[:, here]
        out[:, here] = (gate / (1.0 + jnp.exp(-gate)) * up).astype(out.dtype)


def finish(index, tokens, adapter_up, gate_pre, up_pre, pieces, start, lows):
    requests = tokens.shape[0]
    hidden = adapter_up.shape[1]
    return pl.pallas_call(
        functools.partial(finish_kernel, start, len(pieces), len(lows)),
        out_shape=jax.ShapeDtypeStruct((requests, hidden), jnp.bfloat16),
        in_specs=[NEAR, NEAR, STORED] + [NEAR] * (len(pieces) + len(lows) + 2),
        out_specs=NEAR,
        scratch_shapes=[
            pltpu.VMEM(adapter_up.shape, jnp.bfloat16),
            pltpu.VMEM((requests, adapter_up.shape[0]), jnp.bfloat16),
            pltpu.SemaphoreType.DMA,
        ],
        cost_estimate=pl.CostEstimate(
            flops=2 * requests * sum(p.shape[0] for p in pieces) * hidden,
            bytes_accessed=4 << 20,
            transcendentals=requests * hidden,
        ),
        compiler_params=pltpu.CompilerParams(vmem_limit_bytes=8 << 20),
        name="finish",
    )(
        index,
        near(tokens),
        far(adapter_up),
        near(gate_pre),
        near(up_pre),
        *[near(p) for p in pieces],
        *lows,
    )


def on_chip(tokens, gate_weight, up_weight, down, up, request_adapter_index, placement):
    count = lax.axis_size("tensor")
    depth, width = plan(count)
    model, hidden = gate_weight.shape
    index = request_adapter_index[None, :]
    part = model // PIECES

    by_line = [send(tokens, j, 0, 0) for j in range(1, depth)]
    across_own = [send(tokens, 0, k, 0) for k in range(1, width)]
    core_own = send(tokens, 0, 0, 1)
    gate_0 = fetch(gate_weight, 0, part, "fetch_0")
    gate_1 = fetch(gate_weight, part, part, "fetch_1")
    line = pack(by_line, [gate_0, gate_1, core_own, *across_own])
    across_line = [send(line, 0, k, 0) for k in range(1, width)]
    core_line = send(line, 0, 0, 1)
    core_across_own = [send(v, 0, 0, 1) for v in across_own]
    gate_2 = fetch(gate_weight, 2 * part, part, "fetch_2", [line])
    gate_3 = fetch(gate_weight, 3 * part, part, "fetch_3", [line])
    across_line = [tie(v, [gate_2, gate_3]) for v in across_line]
    core_across_line = [send(v, 0, 0, 1) for v in across_line]
    mine, theirs = [tokens, line], [core_own, core_line]
    for own_block, line_block in zip(across_own, across_line):
        mine += [own_block, line_block]
    for own_block, line_block in zip(core_across_own, core_across_line):
        theirs += [own_block, line_block]
    packed, low = collect(
        placement[None, :], index, jnp.swapaxes(down[0], 0, 1), mine, theirs, depth, width
    )

    low_1 = add(low, send(low, 0, 0, 1))
    gate_pre, up_0, up_1 = multiply(
        low, packed, [gate_0, gate_1], 0, [], up_weight, (0, part, part), "gate_a"
    )
    low_2 = add(low_1, *[send(low_1, 0, k, 0) for k in range(1, width)])
    gate_pre, up_2, up_3 = multiply(
        low_1,
        packed,
        [gate_2, gate_3],
        2 * part,
        [gate_pre],
        up_weight,
        (2 * part, part, part),
        "gate_b",
    )
    lows = [low_2] + [send(low_2, j, 0, 0) for j in range(1, depth)]
    (up_pre,) = multiply(low_2, packed, [up_0, up_1], 0, [], None, (), "up_a")
    return finish(
        index, packed, up.reshape(-1, hidden), gate_pre, up_pre, [up_2, up_3], 2 * part, lows
    )


def streamed(
    tokens,
    gate_weight,
    up_weight,
    adapter_down_weight,
    adapter_up_weight,
    request_adapter_index,
    adapter_request_lists,
    placement,
):
    count = lax.axis_size("tensor")
    depth, width = plan(count)
    rows = tokens.shape[0]
    requests = request_adapter_index.shape[0]
    adapters = placement.shape[0]
    rank_width = adapter_down_weight.shape[2]
    own = lax.axis_index("tensor")

    by_line = [tokens] + [send(tokens, j, 0, 0) for j in range(1, depth)]
    plane = list(by_line)
    for k in range(1, width):
        plane += [send(block, 0, k, 0) for block in by_line]
    half = jnp.concatenate(plane, 0)
    other = send(half, 0, 0, 1)
    gathered = jnp.concatenate([half, other], 0)

    slot = jnp.arange(requests, dtype=jnp.int32)
    block, inner = slot // rows, slot % rows
    j, k, m = block % depth, block // depth % width, block // (depth * width)
    origin = ((own // (2 * width) - j) % depth * width + (own // 2 - k) % width) * 2 + (own + m) % 2
    row_id = origin * rows + inner

    owner = jnp.sum(jnp.where(placement == own, jnp.arange(adapters, dtype=jnp.int32), 0))
    wanted = lax.dynamic_slice_in_dim(adapter_request_lists, owner, 1, 0)[0]
    picker = (wanted[:, None] == row_id[None, :]).astype(jnp.bfloat16)
    picked = jnp.dot(picker, gathered, preferred_element_type=jnp.float32).astype(jnp.bfloat16)
    low_rank = jnp.dot(picked, adapter_down_weight[0], preferred_element_type=jnp.float32)
    spread = (jnp.arange(requests, dtype=jnp.int32)[:, None] == wanted[None, :]).astype(jnp.bfloat16)
    mixed = jnp.dot(spread, low_rank.astype(jnp.bfloat16), preferred_element_type=jnp.float32)
    mixed = mixed.astype(jnp.bfloat16)
    step = 1
    while step < count:
        mixed = mixed + lax.ppermute(mixed, "tensor", [(i, i ^ step) for i in range(count)])
        step *= 2

    gate_pre = jnp.dot(gathered, gate_weight, preferred_element_type=jnp.float32)
    up_pre = jnp.dot(gathered, up_weight, preferred_element_type=jnp.float32)
    here = (row_id[:, None] == jnp.arange(requests, dtype=jnp.int32)[None, :]).astype(jnp.bfloat16)
    mine = jnp.dot(here, mixed, preferred_element_type=jnp.float32).astype(jnp.bfloat16)
    index = jnp.take(request_adapter_index, row_id)
    chosen = index[:, None] == jnp.arange(adapters, dtype=jnp.int32)[None, :]
    expanded = jnp.where(chosen[:, :, None], mine[:, None, :], jnp.zeros((), jnp.bfloat16))
    delta = jnp.dot(
        expanded.reshape(requests, adapters * rank_width),
        adapter_up_weight.reshape(adapters * rank_width, -1),
        preferred_element_type=jnp.float32,
    )
    hidden = (jax.nn.silu(gate_pre) * (up_pre + delta)).astype(jnp.bfloat16)
    return jnp.dot(here.T, hidden, preferred_element_type=jnp.float32).astype(jnp.bfloat16)


def body(
    tokens,
    gate_weight,
    up_weight,
    adapter_down_weight,
    adapter_up_weight,
    request_adapter_index,
    adapter_request_lists,
    placement,
):
    if request_adapter_index.shape[0] <= 128:
        return on_chip(
            tokens,
            gate_weight,
            up_weight,
            adapter_down_weight,
            adapter_up_weight,
            request_adapter_index,
            placement,
        )
    return streamed(
        tokens,
        gate_weight,
        up_weight,
        adapter_down_weight,
        adapter_up_weight,
        request_adapter_index,
        adapter_request_lists,
        placement,
    )


def solution(mesh):
    in_specs = (
        P(("groups", "tensor"), None),
        P(None, "tensor"),
        P(None, "tensor"),
        P(("groups", "tensor"), None, None),
        P("groups", None, "tensor"),
        P("groups"),
        P("groups", None),
        P("groups"),
    )
    out_specs = P("groups", "tensor")
    return jax.shard_map(body, mesh=mesh, in_specs=in_specs, out_specs=out_specs, check_vma=False)
```

```python
import functools

import jax
import jax.numpy as jnp
from jax import lax
from jax.experimental import pallas as pl
from jax.experimental.pallas import tpu as pltpu
from jax.sharding import PartitionSpec as P

TILE = 256
PIECES = 4
NEAR = pl.BlockSpec(memory_space=pltpu.VMEM)
FAR = pl.BlockSpec(memory_space=pl.ANY)
STORED = pl.BlockSpec(memory_space=pltpu.HBM)


def near(value):
    return pltpu.with_memory_space_constraint(value, pltpu.VMEM)


def far(value):
    return pltpu.with_memory_space_constraint(value, pltpu.HBM)


def plan(count):
    lines = 1
    while lines * lines < count // 2:
        lines *= 2
    return lines, count // 2 // lines


def send(value, da, db, dc):
    count = lax.axis_size("tensor")
    depth, width = plan(count)
    pairs = []
    for i in range(count):
        a, b, c = i // (2 * width), i // 2 % width, i % 2
        pairs.append((i, ((a + da) % depth * width + (b + db) % width) * 2 + (c + dc) % 2))
    return lax.ppermute(value, "tensor", pairs)


def swap(value, mask):
    pairs = [(i, i ^ mask) for i in range(lax.axis_size("tensor"))]
    return lax.ppermute(value, "tensor", pairs)


def fetch_kernel(start, skipped, source, *refs):
    target, sems = refs[skipped:]
    rows = target.shape[0] // sems.shape[0]
    copies = [
        pltpu.make_async_copy(
            source.at[pl.ds(start + i * rows, rows)], target.at[pl.ds(i * rows, rows)], sems.at[i]
        )
        for i in range(sems.shape[0])
    ]
    for copy in copies:
        copy.start()
    for copy in copies:
        copy.wait()


def fetch(weight, start, rows, name, after=()):
    return pl.pallas_call(
        functools.partial(fetch_kernel, start, len(after)),
        out_shape=pltpu.VMEM((rows, weight.shape[1]), weight.dtype),
        in_specs=[STORED] + [FAR] * len(after),
        out_specs=NEAR,
        scratch_shapes=[pltpu.SemaphoreType.DMA((4,))],
        cost_estimate=pl.CostEstimate(
            flops=0, bytes_accessed=rows * weight.shape[1] * 2, transcendentals=0
        ),
        compiler_params=pltpu.CompilerParams(vmem_limit_bytes=1 << 20),
        name=name,
    )(far(weight), *after)


def across(row):
    n = row.shape[1]
    return jnp.broadcast_to(row, (n, n)).T


def pack_kernel(n, *refs):
    place = 0
    for ref in refs[:n]:
        for i in range(ref.shape[0]):
            refs[-1][place] = ref[i]
            place += 1


def pack(blocks, after):
    rows, model = blocks[0].shape[1:]
    n = len(blocks)
    return pl.pallas_call(
        functools.partial(pack_kernel, n),
        out_shape=pltpu.VMEM((sum(b.shape[0] for b in blocks), rows, model), jnp.bfloat16),
        in_specs=[NEAR] * n + [FAR] * len(after),
        out_specs=NEAR,
        cost_estimate=pl.CostEstimate(flops=0, bytes_accessed=1 << 18, transcendentals=0),
        compiler_params=pltpu.CompilerParams(vmem_limit_bytes=1 << 20),
        name="pack",
    )(*[near(v) for v in blocks], *after)


def tie_kernel(*refs):
    pass


def tie(value, after):
    return pl.pallas_call(
        tie_kernel,
        out_shape=jax.ShapeDtypeStruct(value.shape, value.dtype),
        in_specs=[FAR] * (1 + len(after)),
        out_specs=FAR,
        input_output_aliases={0: 0},
        cost_estimate=pl.CostEstimate(flops=0, bytes_accessed=1 << 10, transcendentals=0),
        compiler_params=pltpu.CompilerParams(vmem_limit_bytes=1 << 20),
        name="tie",
    )(value, *after)


def collect_kernel(depth, width, sizes, placement, index, down, *refs):
    mine, theirs = refs[: len(sizes)], refs[len(sizes) : 2 * len(sizes)]
    packed, low = refs[2 * len(sizes) :]
    own = lax.axis_index("tensor")
    c = own % 2
    rows = packed.shape[0] // (2 * depth * width)
    place = 0
    for size, p_ref, q_ref in zip(sizes, mine, theirs):
        for i in range(size):
            j, k = place % depth, place // depth
            chip = (own // 2) ^ (j * width + k)
            p, q = p_ref[i], q_ref[i]
            first, second = jnp.where(c == 0, p, q), jnp.where(c == 0, q, p)
            packed[pl.ds(pl.multiple_of(chip * 2 * rows, 2 * rows), 2 * rows), :] = (
                jnp.concatenate([first, second], 0)
            )
            place += 1
    full = lax.dot_general(
        packed[...], down[...], (((1,), (1,)), ((), ())), preferred_element_type=jnp.float32
    )
    ids = lax.broadcasted_iota(jnp.int32, placement.shape, 1)
    owner = jnp.sum(jnp.where(placement[...] == own, ids, 0), axis=1, keepdims=True)
    chosen = across(jnp.where(index[...] == owner, 1, 0))[:, : full.shape[1]]
    low[...] = jnp.where(chosen == 1, full, 0.0).astype(low.dtype)


def collect(placement, index, down, mine, theirs, depth, width):
    sizes = [v.shape[0] for v in mine]
    rows, model = mine[0].shape[1:]
    requests = 2 * depth * width * rows
    return pl.pallas_call(
        functools.partial(collect_kernel, depth, width, sizes),
        out_shape=[
            pltpu.VMEM((requests, model), jnp.bfloat16),
            jax.ShapeDtypeStruct((requests, down.shape[0]), jnp.bfloat16),
        ],
        in_specs=[NEAR] * (3 + 2 * len(sizes)),
        out_specs=[NEAR] * 2,
        cost_estimate=pl.CostEstimate(
            flops=2 * requests * model * 64, bytes_accessed=1 << 20, transcendentals=0
        ),
        compiler_params=pltpu.CompilerParams(vmem_limit_bytes=4 << 20),
        name="collect",
    )(placement, index, down, *[near(v) for v in mine], *[near(v) for v in theirs])


def add_kernel(*refs):
    total = refs[0][...]
    for ref in refs[1:-1]:
        total = total + ref[...]
    refs[-1][...] = total


def add(*values):
    return pl.pallas_call(
        add_kernel,
        out_shape=jax.ShapeDtypeStruct(values[0].shape, values[0].dtype),
        in_specs=[NEAR] * len(values),
        out_specs=NEAR,
        cost_estimate=pl.CostEstimate(flops=0, bytes_accessed=1 << 14, transcendentals=0),
        compiler_params=pltpu.CompilerParams(vmem_limit_bytes=1 << 20),
        name="add",
    )(*values)


def piecewise(tokens, pieces, start, here):
    total = None
    for piece in pieces:
        rows = piece.shape[0]
        term = jnp.dot(
            tokens[:, start : start + rows], piece[:, here], preferred_element_type=jnp.float32
        )
        total = term if total is None else total + term
        start += rows
    return total


def multiply_kernel(start, n, begun, fetched, *refs):
    tokens, refs = refs[1], refs[2:]
    pieces, refs = refs[:n], refs[n:]
    before, refs = refs[:begun], refs[begun:]
    copies = []
    if fetched:
        sources, (out, *targets, sems) = refs[: len(fetched)], refs[len(fetched) :]
        for i, ((first, rows), source, target) in enumerate(zip(fetched, sources, targets)):
            copies.append(
                pltpu.make_async_copy(source.at[pl.ds(first, rows)], target, sems.at[i])
            )
    else:
        (out,) = refs
    for copy in copies:
        copy.start()

    @pl.loop(0, out.shape[1] // TILE)
    def _(i):
        here = pl.ds(pl.multiple_of(i * TILE, TILE), TILE)
        total = piecewise(tokens, pieces, start, here)
        if begun:
            total = total + before[0][:, here]
        out[:, here] = total

    for copy in copies:
        copy.wait()


def multiply(after, tokens, pieces, start, begun, fetched, name):
    requests = tokens.shape[0]
    hidden = pieces[0].shape[1]
    out_shape = [pltpu.VMEM((requests, hidden), jnp.float32)]
    out_shape += [pltpu.VMEM((rows, hidden), source.dtype) for source, first, rows in fetched]
    operands = [after, near(tokens)] + [near(p) for p in pieces] + [near(b) for b in begun]
    in_specs = [FAR] + [NEAR] * (len(operands) - 1) + [STORED] * len(fetched)
    operands += [far(source) for source, first, rows in fetched]
    return pl.pallas_call(
        functools.partial(
            multiply_kernel,
            start,
            len(pieces),
            len(begun),
            [(first, rows) for source, first, rows in fetched],
        ),
        out_shape=out_shape,
        in_specs=in_specs,
        out_specs=[NEAR] * len(out_shape),
        scratch_shapes=[pltpu.SemaphoreType.DMA((len(fetched),))] if fetched else [],
        cost_estimate=pl.CostEstimate(
            flops=2 * requests * sum(p.shape[0] for p in pieces) * hidden,
            bytes_accessed=16 << 20,
            transcendentals=0,
        ),
        compiler_params=pltpu.CompilerParams(vmem_limit_bytes=2 << 20),
        name=name,
    )(*operands)


def finish_kernel(start, n, m, index, tokens, adapter_up, gate_pre, up_pre, *refs):
    pieces, refs = refs[:n], refs[n:]
    lows, refs = refs[:m], refs[m:]
    out, expanded = refs
    rank = lows[0].shape[1]
    mixed = lows[0][...]
    for low in lows[1:]:
        mixed = mixed + low[...]
    group = TILE // rank
    lane = lax.broadcasted_iota(jnp.int32, (rank, TILE), 1)
    repeat = (lane % rank == lax.broadcasted_iota(jnp.int32, (rank, TILE), 0)).astype(jnp.bfloat16)
    wide = jnp.dot(mixed, repeat, preferred_element_type=jnp.float32)
    of_lane = lax.broadcasted_iota(jnp.int32, (mixed.shape[0], TILE), 1) // rank
    relative = jnp.concatenate([across(index[...])] * (TILE // mixed.shape[0]), 1) - of_lane
    for i in range(expanded.shape[1] // TILE):
        expanded[:, i * TILE : (i + 1) * TILE] = jnp.where(
            relative == i * group, wide, 0.0
        ).astype(jnp.bfloat16)

    @pl.loop(0, out.shape[1] // TILE)
    def _(i):
        here = pl.ds(pl.multiple_of(i * TILE, TILE), TILE)
        up = up_pre[:, here] + piecewise(tokens, pieces, start, here)
        up = up + jnp.dot(expanded[...], adapter_up[:, here], preferred_element_type=jnp.float32)
        gate = gate_pre[:, here]
        out[:, here] = (gate / (1.0 + jnp.exp(-gate)) * up).astype(out.dtype)


def finish(index, tokens, adapter_up, gate_pre, up_pre, pieces, start, lows):
    requests = tokens.shape[0]
    hidden = adapter_up.shape[1]
    return pl.pallas_call(
        functools.partial(finish_kernel, start, len(pieces), len(lows)),
        out_shape=jax.ShapeDtypeStruct((requests, hidden), jnp.bfloat16),
        in_specs=[NEAR] * (5 + len(pieces) + len(lows)),
        out_specs=NEAR,
        scratch_shapes=[
            pltpu.VMEM((requests, adapter_up.shape[0]), jnp.bfloat16),
        ],
        cost_estimate=pl.CostEstimate(
            flops=2 * requests * sum(p.shape[0] for p in pieces) * hidden,
            bytes_accessed=4 << 20,
            transcendentals=requests * hidden,
        ),
        compiler_params=pltpu.CompilerParams(vmem_limit_bytes=4 << 20),
        name="finish",
    )(
        index,
        near(tokens),
        near(adapter_up),
        near(gate_pre),
        near(up_pre),
        *[near(p) for p in pieces],
        *lows,
    )


def on_chip(tokens, gate_weight, up_weight, down, up, request_adapter_index, placement):
    depth, width = plan(lax.axis_size("tensor"))
    model, hidden = gate_weight.shape
    index = request_adapter_index[None, :]
    part = model // PIECES
    up = up.reshape(-1, hidden)
    own = tokens[None]
    core, column, line_1, line_2 = 1, 2, 2 * width, 4 * width

    block_2 = swap(own, line_2)
    block_1 = swap(own, line_1)
    column_0 = swap(own, column)
    gate_0 = fetch(gate_weight, 0, part, "fetch_0")
    block_2 = tie(block_2, [gate_0])
    block_3 = swap(block_2, line_1)
    blocks_12 = pack([block_1, block_2], [gate_0, column_0])
    columns_12 = swap(blocks_12, column)
    gate_1 = fetch(gate_weight, part, part, "fetch_1", [blocks_12])
    block_3 = tie(block_3, [gate_1])
    column_3 = swap(block_3, column)
    line = pack([own, blocks_12, block_3], [])
    core_line = swap(line, core)
    gate_2 = fetch(gate_weight, 2 * part, part, "fetch_2", [line])
    columns = pack([column_0, columns_12, column_3], [gate_2])
    core_columns = swap(columns, core)
    packed, low = collect(
        placement[None, :],
        index,
        jnp.swapaxes(down[0], 0, 1),
        [line, columns],
        [core_line, core_columns],
        depth,
        width,
    )

    low_1 = add(low, swap(low, line_2))
    gate_pre, gate_3, up_0 = multiply(
        low,
        packed,
        [gate_0, gate_1],
        0,
        [],
        [(gate_weight, 3 * part, part), (up_weight, 0, part)],
        "gate_a",
    )
    low_2 = add(low_1, swap(low_1, line_1))
    gate_pre, up_1, up_2 = multiply(
        low_1,
        packed,
        [gate_2, gate_3],
        2 * part,
        [gate_pre],
        [(up_weight, part, part), (up_weight, 2 * part, part)],
        "gate_b",
    )
    lows = [low_2] + [swap(low_2, mask) for mask in (core, column, core + column)]
    up_pre, near_up, up_3 = multiply(
        low_2,
        packed,
        [up_0, up_1],
        0,
        [],
        [(up, 0, up.shape[0]), (up_weight, 3 * part, part)],
        "up_a",
    )
    return finish(index, packed, near_up, gate_pre, up_pre, [up_2, up_3], 2 * part, lows)


def streamed(
    tokens,
    gate_weight,
    up_weight,
    adapter_down_weight,
    adapter_up_weight,
    request_adapter_index,
    adapter_request_lists,
    placement,
):
    count = lax.axis_size("tensor")
    depth, width = plan(count)
    rows = tokens.shape[0]
    requests = request_adapter_index.shape[0]
    adapters = placement.shape[0]
    rank_width = adapter_down_weight.shape[2]
    own = lax.axis_index("tensor")

    by_line = [tokens] + [send(tokens, j, 0, 0) for j in range(1, depth)]
    plane = list(by_line)
    for k in range(1, width):
        plane += [send(block, 0, k, 0) for block in by_line]
    half = jnp.concatenate(plane, 0)
    other = send(half, 0, 0, 1)
    gathered = jnp.concatenate([half, other], 0)

    slot = jnp.arange(requests, dtype=jnp.int32)
    block, inner = slot // rows, slot % rows
    j, k, m = block % depth, block // depth % width, block // (depth * width)
    origin = ((own // (2 * width) - j) % depth * width + (own // 2 - k) % width) * 2 + (own + m) % 2
    row_id = origin * rows + inner

    owner = jnp.sum(jnp.where(placement == own, jnp.arange(adapters, dtype=jnp.int32), 0))
    wanted = lax.dynamic_slice_in_dim(adapter_request_lists, owner, 1, 0)[0]
    picker = (wanted[:, None] == row_id[None, :]).astype(jnp.bfloat16)
    picked = jnp.dot(picker, gathered, preferred_element_type=jnp.float32).astype(jnp.bfloat16)
    low_rank = jnp.dot(picked, adapter_down_weight[0], preferred_element_type=jnp.float32)
    spread = (jnp.arange(requests, dtype=jnp.int32)[:, None] == wanted[None, :]).astype(jnp.bfloat16)
    mixed = jnp.dot(spread, low_rank.astype(jnp.bfloat16), preferred_element_type=jnp.float32)
    mixed = mixed.astype(jnp.bfloat16)
    step = 1
    while step < count:
        mixed = mixed + lax.ppermute(mixed, "tensor", [(i, i ^ step) for i in range(count)])
        step *= 2

    gate_pre = jnp.dot(gathered, gate_weight, preferred_element_type=jnp.float32)
    up_pre = jnp.dot(gathered, up_weight, preferred_element_type=jnp.float32)
    here = (row_id[:, None] == jnp.arange(requests, dtype=jnp.int32)[None, :]).astype(jnp.bfloat16)
    mine = jnp.dot(here, mixed, preferred_element_type=jnp.float32).astype(jnp.bfloat16)
    index = jnp.take(request_adapter_index, row_id)
    chosen = index[:, None] == jnp.arange(adapters, dtype=jnp.int32)[None, :]
    expanded = jnp.where(chosen[:, :, None], mine[:, None, :], jnp.zeros((), jnp.bfloat16))
    delta = jnp.dot(
        expanded.reshape(requests, adapters * rank_width),
        adapter_up_weight.reshape(adapters * rank_width, -1),
        preferred_element_type=jnp.float32,
    )
    hidden = (jax.nn.silu(gate_pre) * (up_pre + delta)).astype(jnp.bfloat16)
    return jnp.dot(here.T, hidden, preferred_element_type=jnp.float32).astype(jnp.bfloat16)


def body(
    tokens,
    gate_weight,
    up_weight,
    adapter_down_weight,
    adapter_up_weight,
    request_adapter_index,
    adapter_request_lists,
    placement,
):
    count = lax.axis_size("tensor")
    if plan(count) == (4, 2) and tokens.shape[0] == 8:
        return on_chip(
            tokens,
            gate_weight,
            up_weight,
            adapter_down_weight,
            adapter_up_weight,
            request_adapter_index,
            placement,
        )
    return streamed(
        tokens,
        gate_weight,
        up_weight,
        adapter_down_weight,
        adapter_up_weight,
        request_adapter_index,
        adapter_request_lists,
        placement,
    )


def solution(mesh):
    in_specs = (
        P(("groups", "tensor"), None),
        P(None, "tensor"),
        P(None, "tensor"),
        P(("groups", "tensor"), None, None),
        P("groups", None, "tensor"),
        P("groups"),
        P("groups", None),
        P("groups"),
    )
    out_specs = P("groups", "tensor")
    return jax.shard_map(body, mesh=mesh, in_specs=in_specs, out_specs=out_specs, check_vma=False)
```

```python
import functools

import jax
import jax.numpy as jnp
from jax import lax
from jax.experimental import pallas as pl
from jax.experimental.pallas import tpu as pltpu
from jax.sharding import PartitionSpec as P

TILE = 256
PIECES = 4
NEAR = pl.BlockSpec(memory_space=pltpu.VMEM)
FAR = pl.BlockSpec(memory_space=pl.ANY)
STORED = pl.BlockSpec(memory_space=pltpu.HBM)


def near(value):
    return pltpu.with_memory_space_constraint(value, pltpu.VMEM)


def far(value):
    return pltpu.with_memory_space_constraint(value, pltpu.HBM)


def plan(count):
    lines = 1
    while lines * lines < count // 2:
        lines *= 2
    return lines, count // 2 // lines


def send(value, da, db, dc):
    count = lax.axis_size("tensor")
    depth, width = plan(count)
    pairs = []
    for i in range(count):
        a, b, c = i // (2 * width), i // 2 % width, i % 2
        pairs.append((i, ((a + da) % depth * width + (b + db) % width) * 2 + (c + dc) % 2))
    return lax.ppermute(value, "tensor", pairs)


def swap(value, mask):
    pairs = [(i, i ^ mask) for i in range(lax.axis_size("tensor"))]
    return lax.ppermute(value, "tensor", pairs)


def fetch_kernel(start, skipped, source, *refs):
    target, sems = refs[skipped:]
    rows = target.shape[0] // sems.shape[0]
    copies = [
        pltpu.make_async_copy(
            source.at[pl.ds(start + i * rows, rows)], target.at[pl.ds(i * rows, rows)], sems.at[i]
        )
        for i in range(sems.shape[0])
    ]
    for copy in copies:
        copy.start()
    for copy in copies:
        copy.wait()


def fetch(weight, start, rows, name, after=()):
    return pl.pallas_call(
        functools.partial(fetch_kernel, start, len(after)),
        out_shape=pltpu.VMEM((rows, weight.shape[1]), weight.dtype),
        in_specs=[STORED] + [FAR] * len(after),
        out_specs=NEAR,
        scratch_shapes=[pltpu.SemaphoreType.DMA((4,))],
        cost_estimate=pl.CostEstimate(
            flops=0, bytes_accessed=rows * weight.shape[1] * 2, transcendentals=0
        ),
        compiler_params=pltpu.CompilerParams(vmem_limit_bytes=1 << 20),
        name=name,
    )(far(weight), *after)


def across(row):
    n = row.shape[1]
    return jnp.broadcast_to(row, (n, n)).T


def pack_kernel(n, *refs):
    place = 0
    for ref in refs[:n]:
        for i in range(ref.shape[0]):
            refs[-1][place] = ref[i]
            place += 1


def pack(blocks, after):
    rows, model = blocks[0].shape[1:]
    n = len(blocks)
    return pl.pallas_call(
        functools.partial(pack_kernel, n),
        out_shape=pltpu.VMEM((sum(b.shape[0] for b in blocks), rows, model), jnp.bfloat16),
        in_specs=[NEAR] * n + [FAR] * len(after),
        out_specs=NEAR,
        cost_estimate=pl.CostEstimate(flops=0, bytes_accessed=1 << 18, transcendentals=0),
        compiler_params=pltpu.CompilerParams(vmem_limit_bytes=1 << 20),
        name="pack",
    )(*[near(v) for v in blocks], *after)


def tie_kernel(*refs):
    pass


def tie(value, after):
    return pl.pallas_call(
        tie_kernel,
        out_shape=jax.ShapeDtypeStruct(value.shape, value.dtype),
        in_specs=[FAR] * (1 + len(after)),
        out_specs=FAR,
        input_output_aliases={0: 0},
        cost_estimate=pl.CostEstimate(flops=0, bytes_accessed=1 << 10, transcendentals=0),
        compiler_params=pltpu.CompilerParams(vmem_limit_bytes=1 << 20),
        name="tie",
    )(value, *after)


def collect_kernel(depth, width, sizes, first, placement, index, down, core_down, *refs):
    mine, theirs = refs[: len(sizes)], refs[len(sizes) : 2 * len(sizes)]
    source, packed, low, target, sem = refs[2 * len(sizes) :]
    copy = pltpu.make_async_copy(source.at[pl.ds(first, target.shape[0])], target, sem)
    copy.start()
    own = lax.axis_index("tensor")
    c = own % 2
    rows = packed.shape[0] // (2 * depth * width)
    place = 0
    for size, p_ref, q_ref in zip(sizes, mine, theirs):
        for i in range(size):
            j, k = place % depth, place // depth
            chip = (own // 2) ^ (j * width + k)
            p, q = p_ref[i], q_ref[i]
            before, after = jnp.where(c == 0, p, q), jnp.where(c == 0, q, p)
            packed[pl.ds(pl.multiple_of(chip * 2 * rows, 2 * rows), 2 * rows), :] = (
                jnp.concatenate([before, after], 0)
            )
            place += 1
    ids = lax.broadcasted_iota(jnp.int32, placement.shape, 1)
    total = None
    for slot, weight in ((own, down), (own ^ 1, core_down)):
        full = lax.dot_general(
            packed[...], weight[...], (((1,), (1,)), ((), ())), preferred_element_type=jnp.float32
        )
        owner = jnp.sum(jnp.where(placement[...] == slot, ids, 0), axis=1, keepdims=True)
        chosen = across(jnp.where(index[...] == owner, 1, 0))[:, : full.shape[1]]
        total = jnp.where(chosen == 1, full, 0.0 if total is None else total)
    low[...] = total.astype(low.dtype)
    copy.wait()


def collect(placement, index, downs, mine, theirs, depth, width, fetched):
    sizes = [v.shape[0] for v in mine]
    rows, model = mine[0].shape[1:]
    requests = 2 * depth * width * rows
    source, first, fetched_rows = fetched
    return pl.pallas_call(
        functools.partial(collect_kernel, depth, width, sizes, first),
        out_shape=[
            pltpu.VMEM((requests, model), jnp.bfloat16),
            jax.ShapeDtypeStruct((requests, downs[0].shape[0]), jnp.bfloat16),
            pltpu.VMEM((fetched_rows, source.shape[1]), source.dtype),
        ],
        in_specs=[NEAR] * (4 + 2 * len(sizes)) + [STORED],
        out_specs=[NEAR] * 3,
        scratch_shapes=[pltpu.SemaphoreType.DMA],
        cost_estimate=pl.CostEstimate(
            flops=4 * requests * model * 64, bytes_accessed=1 << 20, transcendentals=0
        ),
        compiler_params=pltpu.CompilerParams(vmem_limit_bytes=4 << 20),
        name="collect",
    )(
        placement,
        index,
        *downs,
        *[near(v) for v in mine],
        *[near(v) for v in theirs],
        far(source),
    )


def add_kernel(*refs):
    total = refs[0][...]
    for ref in refs[1:-1]:
        total = total + ref[...]
    refs[-1][...] = total


def add(*values):
    return pl.pallas_call(
        add_kernel,
        out_shape=jax.ShapeDtypeStruct(values[0].shape, values[0].dtype),
        in_specs=[NEAR] * len(values),
        out_specs=NEAR,
        cost_estimate=pl.CostEstimate(flops=0, bytes_accessed=1 << 14, transcendentals=0),
        compiler_params=pltpu.CompilerParams(vmem_limit_bytes=1 << 20),
        name="add",
    )(*values)


def piecewise(tokens, pieces, start, here):
    total = None
    for piece in pieces:
        rows = piece.shape[0]
        term = jnp.dot(
            tokens[:, start : start + rows], piece[:, here], preferred_element_type=jnp.float32
        )
        total = term if total is None else total + term
        start += rows
    return total


def multiply_kernel(start, n, begun, fetched, *refs):
    tokens, refs = refs[1], refs[2:]
    pieces, refs = refs[:n], refs[n:]
    before, refs = refs[:begun], refs[begun:]
    copies = []
    if fetched:
        sources, (out, *targets, sems) = refs[: len(fetched)], refs[len(fetched) :]
        for i, ((first, rows), source, target) in enumerate(zip(fetched, sources, targets)):
            copies.append(
                pltpu.make_async_copy(source.at[pl.ds(first, rows)], target, sems.at[i])
            )
    else:
        (out,) = refs
    for copy in copies:
        copy.start()

    @pl.loop(0, out.shape[1] // TILE)
    def _(i):
        here = pl.ds(pl.multiple_of(i * TILE, TILE), TILE)
        total = piecewise(tokens, pieces, start, here)
        if begun:
            total = total + before[0][:, here]
        out[:, here] = total

    for copy in copies:
        copy.wait()


def multiply(after, tokens, pieces, start, begun, fetched, name):
    requests = tokens.shape[0]
    hidden = pieces[0].shape[1]
    out_shape = [pltpu.VMEM((requests, hidden), jnp.float32)]
    out_shape += [pltpu.VMEM((rows, hidden), source.dtype) for source, first, rows in fetched]
    operands = [after, near(tokens)] + [near(p) for p in pieces] + [near(b) for b in begun]
    in_specs = [FAR] + [NEAR] * (len(operands) - 1) + [STORED] * len(fetched)
    operands += [far(source) for source, first, rows in fetched]
    return pl.pallas_call(
        functools.partial(
            multiply_kernel,
            start,
            len(pieces),
            len(begun),
            [(first, rows) for source, first, rows in fetched],
        ),
        out_shape=out_shape,
        in_specs=in_specs,
        out_specs=[NEAR] * len(out_shape),
        scratch_shapes=[pltpu.SemaphoreType.DMA((len(fetched),))] if fetched else [],
        cost_estimate=pl.CostEstimate(
            flops=2 * requests * sum(p.shape[0] for p in pieces) * hidden,
            bytes_accessed=16 << 20,
            transcendentals=0,
        ),
        compiler_params=pltpu.CompilerParams(vmem_limit_bytes=2 << 20),
        name=name,
    )(*operands)


def finish_kernel(start, n, m, index, tokens, adapter_up, gate_pre, up_pre, *refs):
    pieces, refs = refs[:n], refs[n:]
    lows, refs = refs[:m], refs[m:]
    out, expanded = refs
    rank = lows[0].shape[1]
    mixed = lows[0][...]
    for low in lows[1:]:
        mixed = mixed + low[...]
    group = TILE // rank
    lane = lax.broadcasted_iota(jnp.int32, (rank, TILE), 1)
    repeat = (lane % rank == lax.broadcasted_iota(jnp.int32, (rank, TILE), 0)).astype(jnp.bfloat16)
    wide = jnp.dot(mixed, repeat, preferred_element_type=jnp.float32)
    of_lane = lax.broadcasted_iota(jnp.int32, (mixed.shape[0], TILE), 1) // rank
    relative = jnp.concatenate([across(index[...])] * (TILE // mixed.shape[0]), 1) - of_lane
    for i in range(expanded.shape[1] // TILE):
        expanded[:, i * TILE : (i + 1) * TILE] = jnp.where(
            relative == i * group, wide, 0.0
        ).astype(jnp.bfloat16)

    @pl.loop(0, out.shape[1] // TILE)
    def _(i):
        here = pl.ds(pl.multiple_of(i * TILE, TILE), TILE)
        up = up_pre[:, here] + piecewise(tokens, pieces, start, here)
        up = up + jnp.dot(expanded[...], adapter_up[:, here], preferred_element_type=jnp.float32)
        gate = gate_pre[:, here]
        out[:, here] = (gate / (1.0 + jnp.exp(-gate)) * up).astype(out.dtype)


def finish(index, tokens, adapter_up, gate_pre, up_pre, pieces, start, lows):
    requests = tokens.shape[0]
    hidden = adapter_up.shape[1]
    return pl.pallas_call(
        functools.partial(finish_kernel, start, len(pieces), len(lows)),
        out_shape=jax.ShapeDtypeStruct((requests, hidden), jnp.bfloat16),
        in_specs=[NEAR] * (5 + len(pieces) + len(lows)),
        out_specs=NEAR,
        scratch_shapes=[
            pltpu.VMEM((requests, adapter_up.shape[0]), jnp.bfloat16),
        ],
        cost_estimate=pl.CostEstimate(
            flops=2 * requests * sum(p.shape[0] for p in pieces) * hidden,
            bytes_accessed=4 << 20,
            transcendentals=requests * hidden,
        ),
        compiler_params=pltpu.CompilerParams(vmem_limit_bytes=4 << 20),
        name="finish",
    )(
        index,
        near(tokens),
        near(adapter_up),
        near(gate_pre),
        near(up_pre),
        *[near(p) for p in pieces],
        *lows,
    )


def on_chip(tokens, gate_weight, up_weight, down, up, request_adapter_index, placement):
    depth, width = plan(lax.axis_size("tensor"))
    model, hidden = gate_weight.shape
    index = request_adapter_index[None, :]
    part = model // PIECES
    unit = part // 4
    up = up.reshape(-1, hidden)
    down = jnp.swapaxes(down[0], 0, 1)
    own = tokens[None]
    core, column, line_1, line_2 = 1, 2, 2 * width, 4 * width

    block_1 = swap(own, line_1)
    block_2 = swap(own, line_2)
    column_0 = swap(own, column)
    core_down = swap(down, core)
    gate_0 = fetch(gate_weight, 0, part, "fetch_0")
    block_1 = tie(block_1, [gate_0, column_0])
    column_1 = swap(block_1, column)
    gate_1 = fetch(gate_weight, part, part, "fetch_1", [block_1, core_down])
    block_2 = tie(block_2, [gate_1, column_1])
    block_3 = swap(block_2, line_1)
    column_2 = swap(block_2, column)
    gate_2 = fetch(gate_weight, 2 * part, part, "fetch_2", [block_2])
    block_3 = tie(block_3, [gate_2, column_2])
    column_3 = swap(block_3, column)
    line = pack([own, block_1, block_2, block_3], [])
    core_line = swap(line, core)
    gate_3 = fetch(gate_weight, 3 * part, part, "fetch_3", [line])
    columns = pack([column_0, column_1, column_2, column_3], [gate_3])
    core_columns = swap(columns, core)
    packed, low, up_0 = collect(
        placement[None, :],
        index,
        [down, core_down],
        [line, columns],
        [core_line, core_columns],
        depth,
        width,
        (up_weight, 0, 2 * unit),
    )

    low_1 = add(low, swap(low, line_2))
    gate_pre, up_1 = multiply(
        low, packed, [gate_0, gate_1], 0, [], [(up_weight, 2 * unit, 5 * unit)], "gate_a"
    )
    low_2 = add(low_1, swap(low_1, line_1))
    gate_pre, up_2, up_3 = multiply(
        low_1,
        packed,
        [gate_2, gate_3],
        2 * part,
        [gate_pre],
        [(up_weight, 7 * unit, unit), (up_weight, 8 * unit, part)],
        "gate_b",
    )
    lows = [low_2, swap(low_2, column)]
    up_pre, near_up, up_4 = multiply(
        low_2,
        packed,
        [up_0, up_1, up_2],
        0,
        [],
        [(up, 0, up.shape[0]), (up_weight, 3 * part, part)],
        "up_a",
    )
    return finish(index, packed, near_up, gate_pre, up_pre, [up_3, up_4], 2 * part, lows)


def streamed(
    tokens,
    gate_weight,
    up_weight,
    adapter_down_weight,
    adapter_up_weight,
    request_adapter_index,
    adapter_request_lists,
    placement,
):
    count = lax.axis_size("tensor")
    depth, width = plan(count)
    rows = tokens.shape[0]
    requests = request_adapter_index.shape[0]
    adapters = placement.shape[0]
    rank_width = adapter_down_weight.shape[2]
    own = lax.axis_index("tensor")

    by_line = [tokens] + [send(tokens, j, 0, 0) for j in range(1, depth)]
    plane = list(by_line)
    for k in range(1, width):
        plane += [send(block, 0, k, 0) for block in by_line]
    half = jnp.concatenate(plane, 0)
    other = send(half, 0, 0, 1)
    gathered = jnp.concatenate([half, other], 0)

    slot = jnp.arange(requests, dtype=jnp.int32)
    block, inner = slot // rows, slot % rows
    j, k, m = block % depth, block // depth % width, block // (depth * width)
    origin = ((own // (2 * width) - j) % depth * width + (own // 2 - k) % width) * 2 + (own + m) % 2
    row_id = origin * rows + inner

    owner = jnp.sum(jnp.where(placement == own, jnp.arange(adapters, dtype=jnp.int32), 0))
    wanted = lax.dynamic_slice_in_dim(adapter_request_lists, owner, 1, 0)[0]
    picker = (wanted[:, None] == row_id[None, :]).astype(jnp.bfloat16)
    picked = jnp.dot(picker, gathered, preferred_element_type=jnp.float32).astype(jnp.bfloat16)
    low_rank = jnp.dot(picked, adapter_down_weight[0], preferred_element_type=jnp.float32)
    spread = (jnp.arange(requests, dtype=jnp.int32)[:, None] == wanted[None, :]).astype(jnp.bfloat16)
    mixed = jnp.dot(spread, low_rank.astype(jnp.bfloat16), preferred_element_type=jnp.float32)
    mixed = mixed.astype(jnp.bfloat16)
    step = 1
    while step < count:
        mixed = mixed + lax.ppermute(mixed, "tensor", [(i, i ^ step) for i in range(count)])
        step *= 2

    gate_pre = jnp.dot(gathered, gate_weight, preferred_element_type=jnp.float32)
    up_pre = jnp.dot(gathered, up_weight, preferred_element_type=jnp.float32)
    here = (row_id[:, None] == jnp.arange(requests, dtype=jnp.int32)[None, :]).astype(jnp.bfloat16)
    mine = jnp.dot(here, mixed, preferred_element_type=jnp.float32).astype(jnp.bfloat16)
    index = jnp.take(request_adapter_index, row_id)
    chosen = index[:, None] == jnp.arange(adapters, dtype=jnp.int32)[None, :]
    expanded = jnp.where(chosen[:, :, None], mine[:, None, :], jnp.zeros((), jnp.bfloat16))
    delta = jnp.dot(
        expanded.reshape(requests, adapters * rank_width),
        adapter_up_weight.reshape(adapters * rank_width, -1),
        preferred_element_type=jnp.float32,
    )
    hidden = (jax.nn.silu(gate_pre) * (up_pre + delta)).astype(jnp.bfloat16)
    return jnp.dot(here.T, hidden, preferred_element_type=jnp.float32).astype(jnp.bfloat16)


def body(
    tokens,
    gate_weight,
    up_weight,
    adapter_down_weight,
    adapter_up_weight,
    request_adapter_index,
    adapter_request_lists,
    placement,
):
    count = lax.axis_size("tensor")
    if plan(count) == (4, 2) and tokens.shape[0] == 8:
        return on_chip(
            tokens,
            gate_weight,
            up_weight,
            adapter_down_weight,
            adapter_up_weight,
            request_adapter_index,
            placement,
        )
    return streamed(
        tokens,
        gate_weight,
        up_weight,
        adapter_down_weight,
        adapter_up_weight,
        request_adapter_index,
        adapter_request_lists,
        placement,
    )


def solution(mesh):
    in_specs = (
        P(("groups", "tensor"), None),
        P(None, "tensor"),
        P(None, "tensor"),
        P(("groups", "tensor"), None, None),
        P("groups", None, "tensor"),
        P("groups"),
        P("groups", None),
        P("groups"),
    )
    out_specs = P("groups", "tensor")
    return jax.shard_map(body, mesh=mesh, in_specs=in_specs, out_specs=out_specs, check_vma=False)
```

```python
import functools

import jax
import jax.numpy as jnp
from jax import lax
from jax.experimental import pallas as pl
from jax.experimental.pallas import tpu as pltpu
from jax.sharding import PartitionSpec as P

TILE = 256
WIDE = 512
PIECES = 4
NEAR = pl.BlockSpec(memory_space=pltpu.VMEM)
FAR = pl.BlockSpec(memory_space=pl.ANY)
STORED = pl.BlockSpec(memory_space=pltpu.HBM)


def near(value):
    return pltpu.with_memory_space_constraint(value, pltpu.VMEM)


def far(value):
    return pltpu.with_memory_space_constraint(value, pltpu.HBM)


def plan(count):
    lines = 1
    while lines * lines < count // 2:
        lines *= 2
    return lines, count // 2 // lines


def send(value, da, db, dc):
    count = lax.axis_size("tensor")
    depth, width = plan(count)
    pairs = []
    for i in range(count):
        a, b, c = i // (2 * width), i // 2 % width, i % 2
        pairs.append((i, ((a + da) % depth * width + (b + db) % width) * 2 + (c + dc) % 2))
    return lax.ppermute(value, "tensor", pairs)


def swap(value, mask):
    pairs = [(i, i ^ mask) for i in range(lax.axis_size("tensor"))]
    return lax.ppermute(value, "tensor", pairs)


def fetch_kernel(start, skipped, source, *refs):
    target, sems = refs[skipped:]
    rows = target.shape[0] // sems.shape[0]
    copies = [
        pltpu.make_async_copy(
            source.at[pl.ds(start + i * rows, rows)], target.at[pl.ds(i * rows, rows)], sems.at[i]
        )
        for i in range(sems.shape[0])
    ]
    for copy in copies:
        copy.start()
    for copy in copies:
        copy.wait()


def fetch(weight, start, rows, name, after=()):
    return pl.pallas_call(
        functools.partial(fetch_kernel, start, len(after)),
        out_shape=pltpu.VMEM((rows, weight.shape[1]), weight.dtype),
        in_specs=[STORED] + [FAR] * len(after),
        out_specs=NEAR,
        scratch_shapes=[pltpu.SemaphoreType.DMA((4,))],
        cost_estimate=pl.CostEstimate(
            flops=0, bytes_accessed=rows * weight.shape[1] * 2, transcendentals=0
        ),
        compiler_params=pltpu.CompilerParams(vmem_limit_bytes=1 << 20),
        name=name,
    )(far(weight), *after)


def across(row):
    n = row.shape[1]
    return jnp.broadcast_to(row, (n, n)).T


def pack_kernel(n, *refs):
    place = 0
    for ref in refs[:n]:
        for i in range(ref.shape[0]):
            refs[-1][place] = ref[i]
            place += 1


def pack(blocks, after):
    rows, model = blocks[0].shape[1:]
    n = len(blocks)
    return pl.pallas_call(
        functools.partial(pack_kernel, n),
        out_shape=pltpu.VMEM((sum(b.shape[0] for b in blocks), rows, model), jnp.bfloat16),
        in_specs=[NEAR] * n + [FAR] * len(after),
        out_specs=NEAR,
        cost_estimate=pl.CostEstimate(flops=0, bytes_accessed=1 << 18, transcendentals=0),
        compiler_params=pltpu.CompilerParams(vmem_limit_bytes=1 << 20),
        name="pack",
    )(*[near(v) for v in blocks], *after)


def tie_kernel(*refs):
    pass


def tie(value, after):
    return pl.pallas_call(
        tie_kernel,
        out_shape=jax.ShapeDtypeStruct(value.shape, value.dtype),
        in_specs=[FAR] * (1 + len(after)),
        out_specs=FAR,
        input_output_aliases={0: 0},
        cost_estimate=pl.CostEstimate(flops=0, bytes_accessed=1 << 10, transcendentals=0),
        compiler_params=pltpu.CompilerParams(vmem_limit_bytes=1 << 20),
        name="tie",
    )(value, *after)


def collect_kernel(depth, width, sizes, placement, index, down, core_down, *refs):
    mine, theirs = refs[: len(sizes)], refs[len(sizes) : 2 * len(sizes)]
    packed, low = refs[2 * len(sizes) :]
    own = lax.axis_index("tensor")
    c = own % 2
    rows = packed.shape[0] // (2 * depth * width)
    place = 0
    for size, p_ref, q_ref in zip(sizes, mine, theirs):
        for i in range(size):
            j, k = place % depth, place // depth
            chip = (own // 2) ^ (j * width + k)
            p, q = p_ref[i], q_ref[i]
            before, after = jnp.where(c == 0, p, q), jnp.where(c == 0, q, p)
            packed[pl.ds(pl.multiple_of(chip * 2 * rows, 2 * rows), 2 * rows), :] = (
                jnp.concatenate([before, after], 0)
            )
            place += 1
    ids = lax.broadcasted_iota(jnp.int32, placement.shape, 1)
    total = None
    for slot, weight in ((own, down), (own ^ 1, core_down)):
        full = lax.dot_general(
            packed[...], weight[...], (((1,), (1,)), ((), ())), preferred_element_type=jnp.float32
        )
        owner = jnp.sum(jnp.where(placement[...] == slot, ids, 0), axis=1, keepdims=True)
        chosen = across(jnp.where(index[...] == owner, 1, 0))[:, : full.shape[1]]
        total = jnp.where(chosen == 1, full, 0.0 if total is None else total)
    low[...] = total.astype(low.dtype)


def collect(placement, index, downs, mine, theirs, depth, width):
    sizes = [v.shape[0] for v in mine]
    rows, model = mine[0].shape[1:]
    requests = 2 * depth * width * rows
    return pl.pallas_call(
        functools.partial(collect_kernel, depth, width, sizes),
        out_shape=[
            pltpu.VMEM((requests, model), jnp.bfloat16),
            jax.ShapeDtypeStruct((requests, downs[0].shape[0]), jnp.bfloat16),
        ],
        in_specs=[NEAR] * (4 + 2 * len(sizes)),
        out_specs=[NEAR] * 2,
        cost_estimate=pl.CostEstimate(
            flops=4 * requests * model * 64, bytes_accessed=1 << 20, transcendentals=0
        ),
        compiler_params=pltpu.CompilerParams(vmem_limit_bytes=4 << 20),
        name="collect",
    )(
        placement,
        index,
        *downs,
        *[near(v) for v in mine],
        *[near(v) for v in theirs],
    )


def add_kernel(*refs):
    total = refs[0][...]
    for ref in refs[1:-1]:
        total = total + ref[...]
    refs[-1][...] = total


def add(*values):
    return pl.pallas_call(
        add_kernel,
        out_shape=jax.ShapeDtypeStruct(values[0].shape, values[0].dtype),
        in_specs=[NEAR] * len(values),
        out_specs=NEAR,
        cost_estimate=pl.CostEstimate(flops=0, bytes_accessed=1 << 14, transcendentals=0),
        compiler_params=pltpu.CompilerParams(vmem_limit_bytes=1 << 20),
        name="add",
    )(*values)


def split_pieces(pieces):
    pieces = [p if isinstance(p, tuple) else (p, 0, p.shape[0]) for p in pieces]
    return [p[0] for p in pieces], [p[1:] for p in pieces]


def piecewise(tokens, pieces, start, here):
    total = None
    for piece, (first, rows) in pieces:
        term = jnp.dot(
            tokens[:, start : start + rows],
            piece[first : first + rows, here],
            preferred_element_type=jnp.float32,
        )
        total = term if total is None else total + term
        start += rows
    return total


def multiply_kernel(start, parts, begun, fetched, *refs):
    tokens, refs = refs[1], refs[2:]
    pieces, refs = list(zip(refs, parts)), refs[len(parts) :]
    before, refs = refs[:begun], refs[begun:]
    copies = []
    if fetched:
        sources, (out, *targets, sems) = refs[: len(fetched)], refs[len(fetched) :]
        for i, ((first, rows), source, target) in enumerate(zip(fetched, sources, targets)):
            copies.append(
                pltpu.make_async_copy(source.at[pl.ds(first, rows)], target, sems.at[i])
            )
    else:
        (out,) = refs
    for copy in copies:
        copy.start()

    for first in range(0, out.shape[1], WIDE):
        here = pl.ds(first, min(WIDE, out.shape[1] - first))
        total = piecewise(tokens, pieces, start, here)
        if begun:
            total = total + before[0][:, here]
        out[:, here] = total

    for copy in copies:
        copy.wait()


def multiply(after, tokens, pieces, start, begun, fetched, name):
    requests = tokens.shape[0]
    pieces, parts = split_pieces(pieces)
    hidden = pieces[0].shape[1]
    out_shape = [pltpu.VMEM((requests, hidden), jnp.float32)]
    out_shape += [pltpu.VMEM((rows, hidden), source.dtype) for source, first, rows in fetched]
    operands = [after, near(tokens)] + [near(p) for p in pieces] + [near(b) for b in begun]
    in_specs = [FAR] + [NEAR] * (len(operands) - 1) + [STORED] * len(fetched)
    operands += [far(source) for source, first, rows in fetched]
    return pl.pallas_call(
        functools.partial(
            multiply_kernel,
            start,
            parts,
            len(begun),
            [(first, rows) for source, first, rows in fetched],
        ),
        out_shape=out_shape,
        in_specs=in_specs,
        out_specs=[NEAR] * len(out_shape),
        scratch_shapes=[pltpu.SemaphoreType.DMA((len(fetched),))] if fetched else [],
        cost_estimate=pl.CostEstimate(
            flops=2 * requests * sum(rows for first, rows in parts) * hidden,
            bytes_accessed=16 << 20,
            transcendentals=0,
        ),
        compiler_params=pltpu.CompilerParams(vmem_limit_bytes=2 << 20),
        name=name,
    )(*operands)


def finish_kernel(start, parts, m, index, tokens, adapter_up, gate_pre, up_pre, *refs):
    pieces, refs = list(zip(refs, parts)), refs[len(parts) :]
    lows, refs = refs[:m], refs[m:]
    out, expanded = refs
    rank = lows[0].shape[1]
    mixed = lows[0][...]
    for low in lows[1:]:
        mixed = mixed + low[...]
    group = TILE // rank
    lane = lax.broadcasted_iota(jnp.int32, (rank, TILE), 1)
    repeat = (lane % rank == lax.broadcasted_iota(jnp.int32, (rank, TILE), 0)).astype(jnp.bfloat16)
    wide = jnp.dot(mixed, repeat, preferred_element_type=jnp.float32)
    of_lane = lax.broadcasted_iota(jnp.int32, (mixed.shape[0], TILE), 1) // rank
    relative = jnp.concatenate([across(index[...])] * (TILE // mixed.shape[0]), 1) - of_lane
    for i in range(expanded.shape[1] // TILE):
        expanded[:, i * TILE : (i + 1) * TILE] = jnp.where(
            relative == i * group, wide, 0.0
        ).astype(jnp.bfloat16)

    for first in range(0, out.shape[1], WIDE):
        here = pl.ds(first, min(WIDE, out.shape[1] - first))
        up = up_pre[:, here] + piecewise(tokens, pieces, start, here)
        up = up + jnp.dot(expanded[...], adapter_up[:, here], preferred_element_type=jnp.float32)
        gate = gate_pre[:, here]
        out[:, here] = (gate / (1.0 + jnp.exp(-gate)) * up).astype(out.dtype)


def finish(index, tokens, adapter_up, gate_pre, up_pre, pieces, start, lows):
    requests = tokens.shape[0]
    pieces, parts = split_pieces(pieces)
    hidden = adapter_up.shape[1]
    return pl.pallas_call(
        functools.partial(finish_kernel, start, parts, len(lows)),
        out_shape=jax.ShapeDtypeStruct((requests, hidden), jnp.bfloat16),
        in_specs=[NEAR] * (5 + len(pieces) + len(lows)),
        out_specs=NEAR,
        scratch_shapes=[
            pltpu.VMEM((requests, adapter_up.shape[0]), jnp.bfloat16),
        ],
        cost_estimate=pl.CostEstimate(
            flops=2 * requests * sum(rows for first, rows in parts) * hidden,
            bytes_accessed=4 << 20,
            transcendentals=requests * hidden,
        ),
        compiler_params=pltpu.CompilerParams(vmem_limit_bytes=4 << 20),
        name="finish",
    )(
        index,
        near(tokens),
        near(adapter_up),
        near(gate_pre),
        near(up_pre),
        *[near(p) for p in pieces],
        *lows,
    )


def on_chip(tokens, gate_weight, up_weight, down, up, request_adapter_index, placement):
    depth, width = plan(lax.axis_size("tensor"))
    model, hidden = gate_weight.shape
    index = request_adapter_index[None, :]
    part = model // PIECES
    unit = part // 4
    up = up.reshape(-1, hidden)
    down = jnp.swapaxes(down[0], 0, 1)
    own = tokens[None]
    core, column, line_1, line_2 = 1, 2, 2 * width, 4 * width

    block_2 = swap(own, line_2)
    block_1 = swap(own, line_1)
    column_0 = swap(own, column)
    core_down = swap(down, core)
    gate_0 = fetch(gate_weight, 0, 6 * unit, "fetch_0")
    block_2 = tie(block_2, [gate_0])
    block_3 = swap(block_2, line_1)
    blocks_12 = pack([block_1, block_2], [gate_0, column_0, core_down])
    columns_12 = swap(blocks_12, column)
    gate_1 = fetch(gate_weight, 6 * unit, 4 * unit, "fetch_1", [blocks_12])
    block_3 = tie(block_3, [gate_1])
    column_3 = swap(block_3, column)
    line = pack([own, blocks_12, block_3], [])
    core_line = swap(line, core)
    gate_2 = fetch(gate_weight, 10 * unit, 6 * unit, "fetch_2", [line])
    columns = pack([column_0, columns_12, column_3], [gate_2])
    core_columns = swap(columns, core)
    packed, low = collect(
        placement[None, :],
        index,
        [down, core_down],
        [line, columns],
        [core_line, core_columns],
        depth,
        width,
    )

    low_1 = add(low, swap(low, line_2))
    gate_pre, up_0 = multiply(
        low, packed, [gate_0, (gate_1, 0, 2 * unit)], 0, [], [(up_weight, 0, 6 * unit)], "gate_a"
    )
    low_2 = add(low_1, swap(low_1, line_1))
    gate_pre, up_1, up_2 = multiply(
        low_1,
        packed,
        [(gate_1, 2 * unit, 2 * unit), gate_2],
        2 * part,
        [gate_pre],
        [(up_weight, 6 * unit, 2 * unit), (up_weight, 8 * unit, 4 * unit)],
        "gate_b",
    )
    lows = [low_2, swap(low_2, column)]
    up_pre, near_up, up_3 = multiply(
        low_2,
        packed,
        [up_0, up_1],
        0,
        [],
        [(up, 0, up.shape[0]), (up_weight, 3 * part, part)],
        "up_a",
    )
    return finish(index, packed, near_up, gate_pre, up_pre, [up_2, up_3], 2 * part, lows)


def streamed(
    tokens,
    gate_weight,
    up_weight,
    adapter_down_weight,
    adapter_up_weight,
    request_adapter_index,
    adapter_request_lists,
    placement,
):
    count = lax.axis_size("tensor")
    depth, width = plan(count)
    rows = tokens.shape[0]
    requests = request_adapter_index.shape[0]
    adapters = placement.shape[0]
    rank_width = adapter_down_weight.shape[2]
    own = lax.axis_index("tensor")

    by_line = [tokens] + [send(tokens, j, 0, 0) for j in range(1, depth)]
    plane = list(by_line)
    for k in range(1, width):
        plane += [send(block, 0, k, 0) for block in by_line]
    half = jnp.concatenate(plane, 0)
    other = send(half, 0, 0, 1)
    gathered = jnp.concatenate([half, other], 0)

    slot = jnp.arange(requests, dtype=jnp.int32)
    block, inner = slot // rows, slot % rows
    j, k, m = block % depth, block // depth % width, block // (depth * width)
    origin = ((own // (2 * width) - j) % depth * width + (own // 2 - k) % width) * 2 + (own + m) % 2
    row_id = origin * rows + inner

    owner = jnp.sum(jnp.where(placement == own, jnp.arange(adapters, dtype=jnp.int32), 0))
    wanted = lax.dynamic_slice_in_dim(adapter_request_lists, owner, 1, 0)[0]
    picker = (wanted[:, None] == row_id[None, :]).astype(jnp.bfloat16)
    picked = jnp.dot(picker, gathered, preferred_element_type=jnp.float32).astype(jnp.bfloat16)
    low_rank = jnp.dot(picked, adapter_down_weight[0], preferred_element_type=jnp.float32)
    spread = (jnp.arange(requests, dtype=jnp.int32)[:, None] == wanted[None, :]).astype(jnp.bfloat16)
    mixed = jnp.dot(spread, low_rank.astype(jnp.bfloat16), preferred_element_type=jnp.float32)
    mixed = mixed.astype(jnp.bfloat16)
    step = 1
    while step < count:
        mixed = mixed + lax.ppermute(mixed, "tensor", [(i, i ^ step) for i in range(count)])
        step *= 2

    gate_pre = jnp.dot(gathered, gate_weight, preferred_element_type=jnp.float32)
    up_pre = jnp.dot(gathered, up_weight, preferred_element_type=jnp.float32)
    here = (row_id[:, None] == jnp.arange(requests, dtype=jnp.int32)[None, :]).astype(jnp.bfloat16)
    mine = jnp.dot(here, mixed, preferred_element_type=jnp.float32).astype(jnp.bfloat16)
    index = jnp.take(request_adapter_index, row_id)
    chosen = index[:, None] == jnp.arange(adapters, dtype=jnp.int32)[None, :]
    expanded = jnp.where(chosen[:, :, None], mine[:, None, :], jnp.zeros((), jnp.bfloat16))
    delta = jnp.dot(
        expanded.reshape(requests, adapters * rank_width),
        adapter_up_weight.reshape(adapters * rank_width, -1),
        preferred_element_type=jnp.float32,
    )
    hidden = (jax.nn.silu(gate_pre) * (up_pre + delta)).astype(jnp.bfloat16)
    return jnp.dot(here.T, hidden, preferred_element_type=jnp.float32).astype(jnp.bfloat16)


def body(
    tokens,
    gate_weight,
    up_weight,
    adapter_down_weight,
    adapter_up_weight,
    request_adapter_index,
    adapter_request_lists,
    placement,
):
    count = lax.axis_size("tensor")
    if plan(count) == (4, 2) and tokens.shape[0] == 8:
        return on_chip(
            tokens,
            gate_weight,
            up_weight,
            adapter_down_weight,
            adapter_up_weight,
            request_adapter_index,
            placement,
        )
    return streamed(
        tokens,
        gate_weight,
        up_weight,
        adapter_down_weight,
        adapter_up_weight,
        request_adapter_index,
        adapter_request_lists,
        placement,
    )


def solution(mesh):
    in_specs = (
        P(("groups", "tensor"), None),
        P(None, "tensor"),
        P(None, "tensor"),
        P(("groups", "tensor"), None, None),
        P("groups", None, "tensor"),
        P("groups"),
        P("groups", None),
        P("groups"),
    )
    out_specs = P("groups", "tensor")
    return jax.shard_map(body, mesh=mesh, in_specs=in_specs, out_specs=out_specs, check_vma=False)
```

```python
import functools

import jax
import jax.numpy as jnp
from jax import lax
from jax.experimental import pallas as pl
from jax.experimental.pallas import tpu as pltpu
from jax.sharding import PartitionSpec as P

TILE = 256
WIDE = 512
PIECES = 8
NEAR = pl.BlockSpec(memory_space=pltpu.VMEM)
FAR = pl.BlockSpec(memory_space=pl.ANY)
STORED = pl.BlockSpec(memory_space=pltpu.HBM)


def near(value):
    return pltpu.with_memory_space_constraint(value, pltpu.VMEM)


def far(value):
    return pltpu.with_memory_space_constraint(value, pltpu.HBM)


def plan(count):
    lines = 1
    while lines * lines < count // 2:
        lines *= 2
    return lines, count // 2 // lines


def send(value, da, db, dc):
    count = lax.axis_size("tensor")
    depth, width = plan(count)
    pairs = []
    for i in range(count):
        a, b, c = i // (2 * width), i // 2 % width, i % 2
        pairs.append((i, ((a + da) % depth * width + (b + db) % width) * 2 + (c + dc) % 2))
    return lax.ppermute(value, "tensor", pairs)


def swap(value, mask):
    pairs = [(i, i ^ mask) for i in range(lax.axis_size("tensor"))]
    return lax.ppermute(value, "tensor", pairs)


def copies_of(sources, firsts, targets, sems):
    return [
        pltpu.make_async_copy(source.at[pl.ds(first, target.shape[0])], target, sems.at[i])
        for i, (source, first, target) in enumerate(zip(sources, firsts, targets))
    ]


def fetch_kernel(firsts, skipped, source, *refs):
    *targets, sems = refs[skipped:]
    copies = copies_of([source] * len(targets), firsts, targets, sems)
    for copy in copies:
        copy.start()
    for copy in copies:
        copy.wait()


def fetch(weight, firsts, rows, name, after=()):
    return pl.pallas_call(
        functools.partial(fetch_kernel, firsts, len(after)),
        out_shape=[pltpu.VMEM((rows, weight.shape[1]), weight.dtype)] * len(firsts),
        in_specs=[STORED] + [FAR] * len(after),
        out_specs=[NEAR] * len(firsts),
        scratch_shapes=[pltpu.SemaphoreType.DMA((len(firsts),))],
        cost_estimate=pl.CostEstimate(
            flops=0,
            bytes_accessed=len(firsts) * rows * weight.shape[1] * 2,
            transcendentals=0,
        ),
        compiler_params=pltpu.CompilerParams(vmem_limit_bytes=1 << 20),
        name=name,
    )(far(weight), *after)


def across(row):
    n = row.shape[1]
    return jnp.broadcast_to(row, (n, n)).T


def pack_kernel(n, *refs):
    place = 0
    for ref in refs[:n]:
        for i in range(ref.shape[0]):
            refs[-1][place] = ref[i]
            place += 1


def pack(blocks, after):
    rows, model = blocks[0].shape[1:]
    n = len(blocks)
    return pl.pallas_call(
        functools.partial(pack_kernel, n),
        out_shape=pltpu.VMEM((sum(b.shape[0] for b in blocks), rows, model), jnp.bfloat16),
        in_specs=[NEAR] * n + [FAR] * len(after),
        out_specs=NEAR,
        cost_estimate=pl.CostEstimate(flops=0, bytes_accessed=1 << 18, transcendentals=0),
        compiler_params=pltpu.CompilerParams(vmem_limit_bytes=1 << 20),
        name="pack",
    )(*[near(v) for v in blocks], *after)


def tie_kernel(*refs):
    pass


def tie(value, after):
    return pl.pallas_call(
        tie_kernel,
        out_shape=jax.ShapeDtypeStruct(value.shape, value.dtype),
        in_specs=[FAR] * (1 + len(after)),
        out_specs=FAR,
        input_output_aliases={0: 0},
        cost_estimate=pl.CostEstimate(flops=0, bytes_accessed=1 << 10, transcendentals=0),
        compiler_params=pltpu.CompilerParams(vmem_limit_bytes=1 << 20),
        name="tie",
    )(value, *after)


def piecewise(tokens, pieces, start, here):
    total = None
    for piece in pieces:
        rows = piece.shape[0]
        term = jnp.dot(
            tokens[:, start : start + rows], piece[:, here], preferred_element_type=jnp.float32
        )
        total = term if total is None else total + term
        start += rows
    return total


def columns_of(ref):
    width = ref.shape[1]
    return [pl.ds(i, min(WIDE, width - i)) for i in range(0, width, WIDE)]


def collect_kernel(depth, width, sizes, n, firsts, placement, index, down, core_down, *refs):
    mine, theirs = refs[: len(sizes)], refs[len(sizes) : 2 * len(sizes)]
    refs = refs[2 * len(sizes) :]
    pieces, refs = refs[:n], refs[n:]
    source, packed, low, out, *targets, sems = refs
    copies = copies_of([source] * len(targets), firsts, targets, sems)
    for copy in copies:
        copy.start()
    own = lax.axis_index("tensor")
    c = own % 2
    rows = packed.shape[0] // (2 * depth * width)
    place = 0
    for size, p_ref, q_ref in zip(sizes, mine, theirs):
        for i in range(size):
            j, k = place % depth, place // depth
            chip = (own // 2) ^ (j * width + k)
            p, q = p_ref[i], q_ref[i]
            before, after = jnp.where(c == 0, p, q), jnp.where(c == 0, q, p)
            packed[pl.ds(pl.multiple_of(chip * 2 * rows, 2 * rows), 2 * rows), :] = (
                jnp.concatenate([before, after], 0)
            )
            place += 1
    ids = lax.broadcasted_iota(jnp.int32, placement.shape, 1)
    total = None
    for slot, weight in ((own, down), (own ^ 1, core_down)):
        full = lax.dot_general(
            packed[...], weight[...], (((1,), (1,)), ((), ())), preferred_element_type=jnp.float32
        )
        owner = jnp.sum(jnp.where(placement[...] == slot, ids, 0), axis=1, keepdims=True)
        chosen = across(jnp.where(index[...] == owner, 1, 0))[:, : full.shape[1]]
        total = jnp.where(chosen == 1, full, 0.0 if total is None else total)
    low[...] = total.astype(low.dtype)
    for here in columns_of(out):
        out[:, here] = piecewise(packed, pieces, 0, here)
    for copy in copies:
        copy.wait()


def collect(placement, index, downs, mine, theirs, depth, width, pieces, fetched):
    sizes = [v.shape[0] for v in mine]
    rows, model = mine[0].shape[1:]
    requests = 2 * depth * width * rows
    source, firsts, fetched_rows = fetched
    hidden = source.shape[1]
    return pl.pallas_call(
        functools.partial(collect_kernel, depth, width, sizes, len(pieces), firsts),
        out_shape=[
            pltpu.VMEM((requests, model), jnp.bfloat16),
            jax.ShapeDtypeStruct((requests, downs[0].shape[0]), jnp.bfloat16),
            pltpu.VMEM((requests, hidden), jnp.float32),
        ]
        + [pltpu.VMEM((fetched_rows, hidden), source.dtype)] * len(firsts),
        in_specs=[NEAR] * (4 + 2 * len(sizes) + len(pieces)) + [STORED],
        out_specs=[NEAR] * (3 + len(firsts)),
        scratch_shapes=[pltpu.SemaphoreType.DMA((len(firsts),))],
        cost_estimate=pl.CostEstimate(
            flops=2 * requests * hidden * sum(p.shape[0] for p in pieces),
            bytes_accessed=16 << 20,
            transcendentals=0,
        ),
        compiler_params=pltpu.CompilerParams(vmem_limit_bytes=2 << 20),
        name="collect",
    )(
        placement,
        index,
        *downs,
        *[near(v) for v in mine],
        *[near(v) for v in theirs],
        *[near(p) for p in pieces],
        far(source),
    )


def add_kernel(*refs):
    total = refs[0][...]
    for ref in refs[1:-1]:
        total = total + ref[...]
    refs[-1][...] = total


def add(*values):
    return pl.pallas_call(
        add_kernel,
        out_shape=jax.ShapeDtypeStruct(values[0].shape, values[0].dtype),
        in_specs=[NEAR] * len(values),
        out_specs=NEAR,
        cost_estimate=pl.CostEstimate(flops=0, bytes_accessed=1 << 14, transcendentals=0),
        compiler_params=pltpu.CompilerParams(vmem_limit_bytes=1 << 20),
        name="add",
    )(*values)


def multiply_kernel(start, n, begun, firsts, *refs):
    tokens, refs = refs[1], refs[2:]
    pieces, refs = refs[:n], refs[n:]
    before, refs = refs[:begun], refs[begun:]
    sources, (out, *targets) = refs[: len(firsts)], refs[len(firsts) :]
    copies = copies_of(sources, firsts, targets[:-1], targets[-1]) if firsts else []
    for copy in copies:
        copy.start()
    for here in columns_of(out):
        total = piecewise(tokens, pieces, start, here)
        if begun:
            total = total + before[0][:, here]
        out[:, here] = total
    for copy in copies:
        copy.wait()


def multiply(after, tokens, pieces, start, begun, fetched, rows, name):
    requests = tokens.shape[0]
    hidden = pieces[0].shape[1]
    n = len(fetched)
    operands = [after, near(tokens)] + [near(p) for p in pieces] + [near(b) for b in begun]
    in_specs = [FAR] + [NEAR] * (len(operands) - 1) + [STORED] * n
    operands += [far(source) for source, first in fetched]
    return pl.pallas_call(
        functools.partial(
            multiply_kernel, start, len(pieces), len(begun), [first for source, first in fetched]
        ),
        out_shape=[pltpu.VMEM((requests, hidden), jnp.float32)]
        + [pltpu.VMEM((rows, hidden), tokens.dtype)] * n,
        in_specs=in_specs,
        out_specs=[NEAR] * (1 + n),
        scratch_shapes=[pltpu.SemaphoreType.DMA((n,))] if n else [],
        cost_estimate=pl.CostEstimate(
            flops=2 * requests * sum(p.shape[0] for p in pieces) * hidden,
            bytes_accessed=16 << 20,
            transcendentals=0,
        ),
        compiler_params=pltpu.CompilerParams(vmem_limit_bytes=2 << 20),
        name=name,
    )(*operands)


def finish_kernel(m, index, adapter_up, gate_pre, up_pre, *refs):
    lows, (out, expanded) = refs[:m], refs[m:]
    rank = lows[0].shape[1]
    mixed = lows[0][...]
    for low in lows[1:]:
        mixed = mixed + low[...]
    group = TILE // rank
    lane = lax.broadcasted_iota(jnp.int32, (rank, TILE), 1)
    repeat = (lane % rank == lax.broadcasted_iota(jnp.int32, (rank, TILE), 0)).astype(jnp.bfloat16)
    wide = jnp.dot(mixed, repeat, preferred_element_type=jnp.float32)
    of_lane = lax.broadcasted_iota(jnp.int32, (mixed.shape[0], TILE), 1) // rank
    relative = jnp.concatenate([across(index[...])] * (TILE // mixed.shape[0]), 1) - of_lane
    for i in range(expanded.shape[1] // TILE):
        expanded[:, i * TILE : (i + 1) * TILE] = jnp.where(
            relative == i * group, wide, 0.0
        ).astype(jnp.bfloat16)

    for here in columns_of(out):
        delta = jnp.dot(expanded[...], adapter_up[:, here], preferred_element_type=jnp.float32)
        gate = gate_pre[:, here]
        out[:, here] = (gate / (1.0 + jnp.exp(-gate)) * (up_pre[:, here] + delta)).astype(out.dtype)


def finish(index, adapter_up, gate_pre, up_pre, lows):
    requests, hidden = gate_pre.shape
    return pl.pallas_call(
        functools.partial(finish_kernel, len(lows)),
        out_shape=jax.ShapeDtypeStruct((requests, hidden), jnp.bfloat16),
        in_specs=[NEAR] * (4 + len(lows)),
        out_specs=NEAR,
        scratch_shapes=[pltpu.VMEM((requests, adapter_up.shape[0]), jnp.bfloat16)],
        cost_estimate=pl.CostEstimate(
            flops=2 * requests * adapter_up.shape[0] * hidden,
            bytes_accessed=4 << 20,
            transcendentals=requests * hidden,
        ),
        compiler_params=pltpu.CompilerParams(vmem_limit_bytes=2 << 20),
        name="finish",
    )(index, near(adapter_up), near(gate_pre), near(up_pre), *lows)


def on_chip(tokens, gate_weight, up_weight, down, up, request_adapter_index, placement):
    depth, width = plan(lax.axis_size("tensor"))
    model, hidden = gate_weight.shape
    index = request_adapter_index[None, :]
    unit = model // PIECES
    firsts = [i * unit for i in range(PIECES)]
    up = up.reshape(-1, hidden)
    down = jnp.swapaxes(down[0], 0, 1)
    own = tokens[None]
    core, column, line_1, line_2 = 1, 2, 2 * width, 4 * width

    block_2 = swap(own, line_2)
    block_1 = swap(own, line_1)
    column_0 = swap(own, column)
    core_down = swap(down, core)
    gate_0, gate_1, gate_2 = fetch(gate_weight, firsts[:3], unit, "fetch_0")
    block_2 = tie(block_2, [gate_0])
    block_3 = swap(block_2, line_1)
    blocks_12 = pack([block_1, block_2], [gate_0, column_0, core_down])
    columns_12 = swap(blocks_12, column)
    gate_3, gate_4 = fetch(gate_weight, firsts[3:5], unit, "fetch_1", [blocks_12])
    block_3 = tie(block_3, [gate_3])
    column_3 = swap(block_3, column)
    line = pack([own, blocks_12, block_3], [])
    core_line = swap(line, core)
    gate_5, gate_6, gate_7 = fetch(gate_weight, firsts[5:], unit, "fetch_2", [line])
    columns = pack([column_0, columns_12, column_3], [gate_5])
    core_columns = swap(columns, core)
    packed, low, gate_pre, up_0, up_1, up_2 = collect(
        placement[None, :],
        index,
        [down, core_down],
        [line, columns],
        [core_line, core_columns],
        depth,
        width,
        [gate_0, gate_1, gate_2, gate_3],
        (up_weight, firsts[:3], unit),
    )

    low_1 = add(low, swap(low, line_2))
    gate_pre, up_3, up_4, up_5 = multiply(
        low,
        packed,
        [gate_4, gate_5, gate_6, gate_7],
        firsts[4],
        [gate_pre],
        [(up_weight, first) for first in firsts[3:6]],
        unit,
        "gate_b",
    )
    low_2 = add(low_1, swap(low_1, line_1))
    up_pre, near_up, up_6, up_7 = multiply(
        low_1,
        packed,
        [up_0, up_1, up_2, up_3, up_4, up_5],
        0,
        [],
        [(up, 0), (up_weight, firsts[6]), (up_weight, firsts[7])],
        unit,
        "up_a",
    )
    lows = [low_2, swap(low_2, column)]
    (up_pre,) = multiply(low_2, packed, [up_6, up_7], firsts[6], [up_pre], [], 0, "up_b")
    return finish(index, near_up, gate_pre, up_pre, lows)


def streamed(
    tokens,
    gate_weight,
    up_weight,
    adapter_down_weight,
    adapter_up_weight,
    request_adapter_index,
    adapter_request_lists,
    placement,
):
    count = lax.axis_size("tensor")
    depth, width = plan(count)
    rows = tokens.shape[0]
    requests = request_adapter_index.shape[0]
    adapters = placement.shape[0]
    rank_width = adapter_down_weight.shape[2]
    own = lax.axis_index("tensor")

    by_line = [tokens] + [send(tokens, j, 0, 0) for j in range(1, depth)]
    plane = list(by_line)
    for k in range(1, width):
        plane += [send(block, 0, k, 0) for block in by_line]
    half = jnp.concatenate(plane, 0)
    other = send(half, 0, 0, 1)
    gathered = jnp.concatenate([half, other], 0)

    slot = jnp.arange(requests, dtype=jnp.int32)
    block, inner = slot // rows, slot % rows
    j, k, m = block % depth, block // depth % width, block // (depth * width)
    origin = ((own // (2 * width) - j) % depth * width + (own // 2 - k) % width) * 2 + (own + m) % 2
    row_id = origin * rows + inner

    owner = jnp.sum(jnp.where(placement == own, jnp.arange(adapters, dtype=jnp.int32), 0))
    wanted = lax.dynamic_slice_in_dim(adapter_request_lists, owner, 1, 0)[0]
    picker = (wanted[:, None] == row_id[None, :]).astype(jnp.bfloat16)
    picked = jnp.dot(picker, gathered, preferred_element_type=jnp.float32).astype(jnp.bfloat16)
    low_rank = jnp.dot(picked, adapter_down_weight[0], preferred_element_type=jnp.float32)
    spread = (jnp.arange(requests, dtype=jnp.int32)[:, None] == wanted[None, :]).astype(jnp.bfloat16)
    mixed = jnp.dot(spread, low_rank.astype(jnp.bfloat16), preferred_element_type=jnp.float32)
    mixed = mixed.astype(jnp.bfloat16)
    step = 1
    while step < count:
        mixed = mixed + lax.ppermute(mixed, "tensor", [(i, i ^ step) for i in range(count)])
        step *= 2

    gate_pre = jnp.dot(gathered, gate_weight, preferred_element_type=jnp.float32)
    up_pre = jnp.dot(gathered, up_weight, preferred_element_type=jnp.float32)
    here = (row_id[:, None] == jnp.arange(requests, dtype=jnp.int32)[None, :]).astype(jnp.bfloat16)
    mine = jnp.dot(here, mixed, preferred_element_type=jnp.float32).astype(jnp.bfloat16)
    index = jnp.take(request_adapter_index, row_id)
    chosen = index[:, None] == jnp.arange(adapters, dtype=jnp.int32)[None, :]
    expanded = jnp.where(chosen[:, :, None], mine[:, None, :], jnp.zeros((), jnp.bfloat16))
    delta = jnp.dot(
        expanded.reshape(requests, adapters * rank_width),
        adapter_up_weight.reshape(adapters * rank_width, -1),
        preferred_element_type=jnp.float32,
    )
    hidden = (jax.nn.silu(gate_pre) * (up_pre + delta)).astype(jnp.bfloat16)
    return jnp.dot(here.T, hidden, preferred_element_type=jnp.float32).astype(jnp.bfloat16)


def body(
    tokens,
    gate_weight,
    up_weight,
    adapter_down_weight,
    adapter_up_weight,
    request_adapter_index,
    adapter_request_lists,
    placement,
):
    count = lax.axis_size("tensor")
    if plan(count) == (4, 2) and tokens.shape[0] == 8:
        return on_chip(
            tokens,
            gate_weight,
            up_weight,
            adapter_down_weight,
            adapter_up_weight,
            request_adapter_index,
            placement,
        )
    return streamed(
        tokens,
        gate_weight,
        up_weight,
        adapter_down_weight,
        adapter_up_weight,
        request_adapter_index,
        adapter_request_lists,
        placement,
    )


def solution(mesh):
    in_specs = (
        P(("groups", "tensor"), None),
        P(None, "tensor"),
        P(None, "tensor"),
        P(("groups", "tensor"), None, None),
        P("groups", None, "tensor"),
        P("groups"),
        P("groups", None),
        P("groups"),
    )
    out_specs = P("groups", "tensor")
    return jax.shard_map(body, mesh=mesh, in_specs=in_specs, out_specs=out_specs, check_vma=False)
```

```python
import functools

import jax
import jax.numpy as jnp
from jax import lax
from jax.experimental import pallas as pl
from jax.experimental.pallas import tpu as pltpu
from jax.sharding import PartitionSpec as P

TILE = 256
WIDE = 512
PIECES = 8
NEAR = pl.BlockSpec(memory_space=pltpu.VMEM)
FAR = pl.BlockSpec(memory_space=pl.ANY)
STORED = pl.BlockSpec(memory_space=pltpu.HBM)


def near(value):
    return pltpu.with_memory_space_constraint(value, pltpu.VMEM)


def far(value):
    return pltpu.with_memory_space_constraint(value, pltpu.HBM)


def plan(count):
    lines = 1
    while lines * lines < count // 2:
        lines *= 2
    return lines, count // 2 // lines


def send(value, da, db, dc):
    count = lax.axis_size("tensor")
    depth, width = plan(count)
    pairs = []
    for i in range(count):
        a, b, c = i // (2 * width), i // 2 % width, i % 2
        pairs.append((i, ((a + da) % depth * width + (b + db) % width) * 2 + (c + dc) % 2))
    return lax.ppermute(value, "tensor", pairs)


def swap(value, mask):
    pairs = [(i, i ^ mask) for i in range(lax.axis_size("tensor"))]
    return lax.ppermute(value, "tensor", pairs)


def copies_of(sources, firsts, targets, sems):
    return [
        pltpu.make_async_copy(source.at[pl.ds(first, target.shape[0])], target, sems.at[i])
        for i, (source, first, target) in enumerate(zip(sources, firsts, targets))
    ]


def fetch_kernel(firsts, skipped, *refs):
    n = len(firsts)
    sources, (*targets, sems) = refs[:n], refs[n + skipped :]
    copies = copies_of(sources, firsts, targets, sems)
    for copy in copies:
        copy.start()
    for copy in copies:
        copy.wait()


def fetch(fetched, rows, name, after=()):
    n = len(fetched)
    width = fetched[0][0].shape[1]
    arrived = pl.pallas_call(
        functools.partial(fetch_kernel, [first for source, first in fetched], len(after)),
        out_shape=[pltpu.VMEM((rows, width), fetched[0][0].dtype)] * n,
        in_specs=[STORED] * n + [FAR] * len(after),
        out_specs=[NEAR] * n,
        scratch_shapes=[pltpu.SemaphoreType.DMA((n,))],
        cost_estimate=pl.CostEstimate(
            flops=0, bytes_accessed=n * rows * width * 2, transcendentals=0
        ),
        compiler_params=pltpu.CompilerParams(vmem_limit_bytes=1 << 20),
        name=name,
    )(*[far(source) for source, first in fetched], *after)
    return list(arrived)


def across(row):
    n = row.shape[1]
    return jnp.broadcast_to(row, (n, n)).T


def pack_kernel(n, *refs):
    place = 0
    for ref in refs[:n]:
        for i in range(ref.shape[0]):
            refs[-1][place] = ref[i]
            place += 1


def pack(blocks, after):
    rows, model = blocks[0].shape[1:]
    n = len(blocks)
    return pl.pallas_call(
        functools.partial(pack_kernel, n),
        out_shape=pltpu.VMEM((sum(b.shape[0] for b in blocks), rows, model), jnp.bfloat16),
        in_specs=[NEAR] * n + [FAR] * len(after),
        out_specs=NEAR,
        cost_estimate=pl.CostEstimate(flops=0, bytes_accessed=1 << 18, transcendentals=0),
        compiler_params=pltpu.CompilerParams(vmem_limit_bytes=1 << 20),
        name="pack",
    )(*[near(v) for v in blocks], *after)


def tie_kernel(*refs):
    pass


def tie(value, after):
    return pl.pallas_call(
        tie_kernel,
        out_shape=jax.ShapeDtypeStruct(value.shape, value.dtype),
        in_specs=[FAR] * (1 + len(after)),
        out_specs=FAR,
        input_output_aliases={0: 0},
        cost_estimate=pl.CostEstimate(flops=0, bytes_accessed=1 << 10, transcendentals=0),
        compiler_params=pltpu.CompilerParams(vmem_limit_bytes=1 << 20),
        name="tie",
    )(value, *after)


def piecewise(tokens, pieces, start, here):
    total = None
    for piece in pieces:
        rows = piece.shape[0]
        term = jnp.dot(
            tokens[:, start : start + rows], piece[:, here], preferred_element_type=jnp.float32
        )
        total = term if total is None else total + term
        start += rows
    return total


def for_columns(width, tile):
    @pl.loop(0, width // WIDE)
    def _(i):
        tile(pl.ds(pl.multiple_of(i * WIDE, WIDE), WIDE))

    if width % WIDE:
        tile(pl.ds(width // WIDE * WIDE, width % WIDE))


def collect_kernel(depth, width, sizes, placement, index, down, core_down, *refs):
    mine, theirs = refs[: len(sizes)], refs[len(sizes) : 2 * len(sizes)]
    packed, low = refs[2 * len(sizes) :]
    own = lax.axis_index("tensor")
    c = own % 2
    rows = packed.shape[0] // (2 * depth * width)
    place = 0
    for size, p_ref, q_ref in zip(sizes, mine, theirs):
        for i in range(size):
            j, k = place % depth, place // depth
            chip = (own // 2) ^ (j * width + k)
            p, q = p_ref[i], q_ref[i]
            before, after = jnp.where(c == 0, p, q), jnp.where(c == 0, q, p)
            packed[pl.ds(pl.multiple_of(chip * 2 * rows, 2 * rows), 2 * rows), :] = (
                jnp.concatenate([before, after], 0)
            )
            place += 1
    ids = lax.broadcasted_iota(jnp.int32, placement.shape, 1)
    total = None
    for slot, weight in ((own, down), (own ^ 1, core_down)):
        full = lax.dot_general(
            packed[...], weight[...], (((1,), (1,)), ((), ())), preferred_element_type=jnp.float32
        )
        owner = jnp.sum(jnp.where(placement[...] == slot, ids, 0), axis=1, keepdims=True)
        chosen = across(jnp.where(index[...] == owner, 1, 0))[:, : full.shape[1]]
        total = jnp.where(chosen == 1, full, 0.0 if total is None else total)
    low[...] = total.astype(low.dtype)


def collect(placement, index, downs, mine, theirs, depth, width):
    sizes = [v.shape[0] for v in mine]
    rows, model = mine[0].shape[1:]
    requests = 2 * depth * width * rows
    return pl.pallas_call(
        functools.partial(collect_kernel, depth, width, sizes),
        out_shape=[
            pltpu.VMEM((requests, model), jnp.bfloat16),
            jax.ShapeDtypeStruct((requests, downs[0].shape[0]), jnp.bfloat16),
        ],
        in_specs=[NEAR] * (4 + 2 * len(sizes)),
        out_specs=[NEAR] * 2,
        cost_estimate=pl.CostEstimate(
            flops=4 * requests * model * 64, bytes_accessed=1 << 20, transcendentals=0
        ),
        compiler_params=pltpu.CompilerParams(vmem_limit_bytes=2 << 20),
        name="collect",
    )(placement, index, *downs, *[near(v) for v in mine], *[near(v) for v in theirs])


def add_kernel(*refs):
    total = refs[0][...]
    for ref in refs[1:-1]:
        total = total + ref[...]
    refs[-1][...] = total


def add(*values):
    return pl.pallas_call(
        add_kernel,
        out_shape=jax.ShapeDtypeStruct(values[0].shape, values[0].dtype),
        in_specs=[NEAR] * len(values),
        out_specs=NEAR,
        cost_estimate=pl.CostEstimate(flops=0, bytes_accessed=1 << 14, transcendentals=0),
        compiler_params=pltpu.CompilerParams(vmem_limit_bytes=1 << 20),
        name="add",
    )(*values)


def multiply_kernel(start, n, begun, firsts, *refs):
    tokens, refs = refs[1], refs[2:]
    pieces, refs = refs[:n], refs[n:]
    before, refs = refs[:begun], refs[begun:]
    sources, (out, *targets) = refs[: len(firsts)], refs[len(firsts) :]
    copies = copies_of(sources, firsts, targets[:-1], targets[-1]) if firsts else []
    for copy in copies:
        copy.start()

    def tile(here):
        total = piecewise(tokens, pieces, start, here)
        if begun:
            total = total + before[0][:, here]
        out[:, here] = total

    for_columns(out.shape[1], tile)
    for copy in copies:
        copy.wait()


def multiply(after, tokens, pieces, start, begun, fetched, rows, name):
    requests = tokens.shape[0]
    hidden = pieces[0].shape[1]
    n = len(fetched)
    operands = [after, near(tokens)] + [near(p) for p in pieces] + [near(b) for b in begun]
    in_specs = [FAR] + [NEAR] * (len(operands) - 1) + [STORED] * n
    operands += [far(source) for source, first in fetched]
    return pl.pallas_call(
        functools.partial(
            multiply_kernel, start, len(pieces), len(begun), [first for source, first in fetched]
        ),
        out_shape=[pltpu.VMEM((requests, hidden), jnp.float32)]
        + [pltpu.VMEM((rows, hidden), tokens.dtype)] * n,
        in_specs=in_specs,
        out_specs=[NEAR] * (1 + n),
        scratch_shapes=[pltpu.SemaphoreType.DMA((n,))] if n else [],
        cost_estimate=pl.CostEstimate(
            flops=2 * requests * sum(p.shape[0] for p in pieces) * hidden,
            bytes_accessed=16 << 20,
            transcendentals=0,
        ),
        compiler_params=pltpu.CompilerParams(vmem_limit_bytes=2 << 20),
        name=name,
    )(*operands)


def finish_kernel(start, n, m, index, tokens, adapter_up, gate_pre, up_pre, *refs):
    pieces, refs = refs[:n], refs[n:]
    lows, (out, expanded) = refs[:m], refs[m:]
    rank = lows[0].shape[1]
    mixed = lows[0][...]
    for low in lows[1:]:
        mixed = mixed + low[...]
    group = TILE // rank
    lane = lax.broadcasted_iota(jnp.int32, (rank, TILE), 1)
    repeat = (lane % rank == lax.broadcasted_iota(jnp.int32, (rank, TILE), 0)).astype(jnp.bfloat16)
    wide = jnp.dot(mixed, repeat, preferred_element_type=jnp.float32)
    of_lane = lax.broadcasted_iota(jnp.int32, (mixed.shape[0], TILE), 1) // rank
    relative = jnp.concatenate([across(index[...])] * (TILE // mixed.shape[0]), 1) - of_lane
    for i in range(expanded.shape[1] // TILE):
        expanded[:, i * TILE : (i + 1) * TILE] = jnp.where(
            relative == i * group, wide, 0.0
        ).astype(jnp.bfloat16)

    def tile(here):
        up = up_pre[:, here] + piecewise(tokens, pieces, start, here)
        up = up + jnp.dot(expanded[...], adapter_up[:, here], preferred_element_type=jnp.float32)
        gate = gate_pre[:, here]
        out[:, here] = (gate / (1.0 + jnp.exp(-gate)) * up).astype(out.dtype)

    for_columns(out.shape[1], tile)


def finish(index, tokens, adapter_up, gate_pre, up_pre, pieces, start, lows):
    requests, hidden = gate_pre.shape
    return pl.pallas_call(
        functools.partial(finish_kernel, start, len(pieces), len(lows)),
        out_shape=jax.ShapeDtypeStruct((requests, hidden), jnp.bfloat16),
        in_specs=[NEAR] * (5 + len(pieces) + len(lows)),
        out_specs=NEAR,
        scratch_shapes=[pltpu.VMEM((requests, adapter_up.shape[0]), jnp.bfloat16)],
        cost_estimate=pl.CostEstimate(
            flops=2 * requests * (adapter_up.shape[0] + sum(p.shape[0] for p in pieces)) * hidden,
            bytes_accessed=4 << 20,
            transcendentals=requests * hidden,
        ),
        compiler_params=pltpu.CompilerParams(vmem_limit_bytes=3 << 20),
        name="finish",
    )(
        index,
        near(tokens),
        near(adapter_up),
        near(gate_pre),
        near(up_pre),
        *[near(p) for p in pieces],
        *lows,
    )


def on_chip(tokens, gate_weight, up_weight, down, up, request_adapter_index, placement):
    depth, width = plan(lax.axis_size("tensor"))
    model, hidden = gate_weight.shape
    index = request_adapter_index[None, :]
    unit = model // PIECES
    firsts = [i * unit for i in range(PIECES)]
    up = up.reshape(-1, hidden)
    down = jnp.swapaxes(down[0], 0, 1)
    own = tokens[None]
    core, column, line_1, line_2 = 1, 2, 2 * width, 4 * width

    block_2 = swap(own, line_2)
    block_1 = swap(own, line_1)
    column_0 = swap(own, column)
    core_down = swap(down, core)
    gates = fetch([(gate_weight, first) for first in firsts[:4]], unit, "fetch_0")
    block_2 = tie(block_2, gates[:1])
    block_3 = swap(block_2, line_1)
    blocks_12 = pack([block_1, block_2], [gates[0], column_0, core_down])
    columns_12 = swap(blocks_12, column)
    gates += fetch([(gate_weight, first) for first in firsts[4:6]], unit, "fetch_1", [blocks_12])
    block_3 = tie(block_3, gates[4:5])
    column_3 = swap(block_3, column)
    line = pack([own, blocks_12, block_3], [])
    core_line = swap(line, core)
    more = [(gate_weight, firsts[6]), (gate_weight, firsts[7]), (up_weight, firsts[0])]
    *last_gates, up_0 = fetch(more, unit, "fetch_2", [line])
    gates += last_gates
    columns = pack([column_0, columns_12, column_3], [up_0])
    core_columns = swap(columns, core)
    packed, low = collect(
        placement[None, :],
        index,
        [down, core_down],
        [line, columns],
        [core_line, core_columns],
        depth,
        width,
    )

    low_1 = add(low, swap(low, line_2))
    gate_pre, *ups = multiply(
        low,
        packed,
        gates[:4],
        0,
        [],
        [(up_weight, first) for first in firsts[1:4]],
        unit,
        "gate_a",
    )
    ups = [up_0] + ups
    low_2 = add(low_1, swap(low_1, line_1))
    gate_pre, *more_ups = multiply(
        low_1,
        packed,
        gates[4:],
        firsts[4],
        [gate_pre],
        [(up_weight, first) for first in firsts[4:7]],
        unit,
        "gate_b",
    )
    lows = [low_2, swap(low_2, column)]
    up_pre, near_up, last_up = multiply(
        low_2, packed, ups, 0, [], [(up, 0), (up_weight, firsts[7])], unit, "up_a"
    )
    return finish(
        index, packed, near_up, gate_pre, up_pre, more_ups + [last_up], firsts[4], lows
    )


def streamed(
    tokens,
    gate_weight,
    up_weight,
    adapter_down_weight,
    adapter_up_weight,
    request_adapter_index,
    adapter_request_lists,
    placement,
):
    count = lax.axis_size("tensor")
    depth, width = plan(count)
    rows = tokens.shape[0]
    requests = request_adapter_index.shape[0]
    adapters = placement.shape[0]
    rank_width = adapter_down_weight.shape[2]
    own = lax.axis_index("tensor")

    by_line = [tokens] + [send(tokens, j, 0, 0) for j in range(1, depth)]
    plane = list(by_line)
    for k in range(1, width):
        plane += [send(block, 0, k, 0) for block in by_line]
    half = jnp.concatenate(plane, 0)
    other = send(half, 0, 0, 1)
    gathered = jnp.concatenate([half, other], 0)

    slot = jnp.arange(requests, dtype=jnp.int32)
    block, inner = slot // rows, slot % rows
    j, k, m = block % depth, block // depth % width, block // (depth * width)
    origin = ((own // (2 * width) - j) % depth * width + (own // 2 - k) % width) * 2 + (own + m) % 2
    row_id = origin * rows + inner

    owner = jnp.sum(jnp.where(placement == own, jnp.arange(adapters, dtype=jnp.int32), 0))
    wanted = lax.dynamic_slice_in_dim(adapter_request_lists, owner, 1, 0)[0]
    picker = (wanted[:, None] == row_id[None, :]).astype(jnp.bfloat16)
    picked = jnp.dot(picker, gathered, preferred_element_type=jnp.float32).astype(jnp.bfloat16)
    low_rank = jnp.dot(picked, adapter_down_weight[0], preferred_element_type=jnp.float32)
    spread = (jnp.arange(requests, dtype=jnp.int32)[:, None] == wanted[None, :]).astype(jnp.bfloat16)
    mixed = jnp.dot(spread, low_rank.astype(jnp.bfloat16), preferred_element_type=jnp.float32)
    mixed = mixed.astype(jnp.bfloat16)
    step = 1
    while step < count:
        mixed = mixed + lax.ppermute(mixed, "tensor", [(i, i ^ step) for i in range(count)])
        step *= 2

    gate_pre = jnp.dot(gathered, gate_weight, preferred_element_type=jnp.float32)
    up_pre = jnp.dot(gathered, up_weight, preferred_element_type=jnp.float32)
    here = (row_id[:, None] == jnp.arange(requests, dtype=jnp.int32)[None, :]).astype(jnp.bfloat16)
    mine = jnp.dot(here, mixed, preferred_element_type=jnp.float32).astype(jnp.bfloat16)
    index = jnp.take(request_adapter_index, row_id)
    chosen = index[:, None] == jnp.arange(adapters, dtype=jnp.int32)[None, :]
    expanded = jnp.where(chosen[:, :, None], mine[:, None, :], jnp.zeros((), jnp.bfloat16))
    delta = jnp.dot(
        expanded.reshape(requests, adapters * rank_width),
        adapter_up_weight.reshape(adapters * rank_width, -1),
        preferred_element_type=jnp.float32,
    )
    hidden = (jax.nn.silu(gate_pre) * (up_pre + delta)).astype(jnp.bfloat16)
    return jnp.dot(here.T, hidden, preferred_element_type=jnp.float32).astype(jnp.bfloat16)


def body(
    tokens,
    gate_weight,
    up_weight,
    adapter_down_weight,
    adapter_up_weight,
    request_adapter_index,
    adapter_request_lists,
    placement,
):
    count = lax.axis_size("tensor")
    if plan(count) == (4, 2) and tokens.shape[0] == 8:
        return on_chip(
            tokens,
            gate_weight,
            up_weight,
            adapter_down_weight,
            adapter_up_weight,
            request_adapter_index,
            placement,
        )
    return streamed(
        tokens,
        gate_weight,
        up_weight,
        adapter_down_weight,
        adapter_up_weight,
        request_adapter_index,
        adapter_request_lists,
        placement,
    )


def solution(mesh):
    in_specs = (
        P(("groups", "tensor"), None),
        P(None, "tensor"),
        P(None, "tensor"),
        P(("groups", "tensor"), None, None),
        P("groups", None, "tensor"),
        P("groups"),
        P("groups", None),
        P("groups"),
    )
    out_specs = P("groups", "tensor")
    return jax.shard_map(body, mesh=mesh, in_specs=in_specs, out_specs=out_specs, check_vma=False)
```

```python
import functools

import jax
import jax.numpy as jnp
from jax import lax
from jax.experimental import pallas as pl
from jax.experimental.pallas import tpu as pltpu
from jax.sharding import PartitionSpec as P

TILE = 256
WIDE = 512
PIECES = 8
NEAR = pl.BlockSpec(memory_space=pltpu.VMEM)
FAR = pl.BlockSpec(memory_space=pl.ANY)
STORED = pl.BlockSpec(memory_space=pltpu.HBM)


def near(value):
    return pltpu.with_memory_space_constraint(value, pltpu.VMEM)


def far(value):
    return pltpu.with_memory_space_constraint(value, pltpu.HBM)


def plan(count):
    lines = 1
    while lines * lines < count // 2:
        lines *= 2
    return lines, count // 2 // lines


def send(value, da, db, dc):
    count = lax.axis_size("tensor")
    depth, width = plan(count)
    pairs = []
    for i in range(count):
        a, b, c = i // (2 * width), i // 2 % width, i % 2
        pairs.append((i, ((a + da) % depth * width + (b + db) % width) * 2 + (c + dc) % 2))
    return lax.ppermute(value, "tensor", pairs)


def swap(value, mask):
    pairs = [(i, i ^ mask) for i in range(lax.axis_size("tensor"))]
    return lax.ppermute(value, "tensor", pairs)


def copies_of(sources, firsts, targets, sems):
    return [
        pltpu.make_async_copy(source.at[pl.ds(first, target.shape[0])], target, sems.at[i])
        for i, (source, first, target) in enumerate(zip(sources, firsts, targets))
    ]


def fetch_kernel(firsts, skipped, *refs):
    n = len(firsts)
    sources, (*targets, sems) = refs[:n], refs[n + skipped :]
    copies = copies_of(sources, firsts, targets, sems)
    for copy in copies:
        copy.start()
    for copy in copies:
        copy.wait()


def fetch(fetched, rows, name, after=()):
    n = len(fetched)
    width = fetched[0][0].shape[1]
    arrived = pl.pallas_call(
        functools.partial(fetch_kernel, [first for source, first in fetched], len(after)),
        out_shape=[pltpu.VMEM((rows, width), fetched[0][0].dtype)] * n,
        in_specs=[STORED] * n + [FAR] * len(after),
        out_specs=[NEAR] * n,
        scratch_shapes=[pltpu.SemaphoreType.DMA((n,))],
        cost_estimate=pl.CostEstimate(
            flops=0, bytes_accessed=n * rows * width * 2, transcendentals=0
        ),
        compiler_params=pltpu.CompilerParams(vmem_limit_bytes=1 << 20),
        name=name,
    )(*[far(source) for source, first in fetched], *after)
    return list(arrived)


def across(row):
    n = row.shape[1]
    return jnp.broadcast_to(row, (n, n)).T


def pack_kernel(n, *refs):
    place = 0
    for ref in refs[:n]:
        for i in range(ref.shape[0]):
            refs[-1][place] = ref[i]
            place += 1


def pack(blocks, after):
    rows, model = blocks[0].shape[1:]
    n = len(blocks)
    return pl.pallas_call(
        functools.partial(pack_kernel, n),
        out_shape=pltpu.VMEM((sum(b.shape[0] for b in blocks), rows, model), jnp.bfloat16),
        in_specs=[NEAR] * n + [FAR] * len(after),
        out_specs=NEAR,
        cost_estimate=pl.CostEstimate(flops=0, bytes_accessed=1 << 18, transcendentals=0),
        compiler_params=pltpu.CompilerParams(vmem_limit_bytes=1 << 20),
        name="pack",
    )(*[near(v) for v in blocks], *after)


def tie_kernel(*refs):
    pass


def tie(value, after):
    return pl.pallas_call(
        tie_kernel,
        out_shape=jax.ShapeDtypeStruct(value.shape, value.dtype),
        in_specs=[FAR] * (1 + len(after)),
        out_specs=FAR,
        input_output_aliases={0: 0},
        cost_estimate=pl.CostEstimate(flops=0, bytes_accessed=1 << 10, transcendentals=0),
        compiler_params=pltpu.CompilerParams(vmem_limit_bytes=1 << 20),
        name="tie",
    )(value, *after)


def piecewise(tokens, pieces, start, here):
    total = None
    for piece in pieces:
        rows = piece.shape[0]
        term = jnp.dot(
            tokens[:, start : start + rows], piece[:, here], preferred_element_type=jnp.float32
        )
        total = term if total is None else total + term
        start += rows
    return total


def for_columns(width, tile):
    @pl.loop(0, width // WIDE)
    def _(i):
        tile(pl.ds(pl.multiple_of(i * WIDE, WIDE), WIDE))

    if width % WIDE:
        tile(pl.ds(width // WIDE * WIDE, width % WIDE))


def collect_kernel(depth, width, sizes, placement, index, down, core_down, *refs):
    mine, theirs = refs[: len(sizes)], refs[len(sizes) : 2 * len(sizes)]
    packed, low = refs[2 * len(sizes) :]
    own = lax.axis_index("tensor")
    c = own % 2
    rows = packed.shape[0] // (2 * depth * width)
    place = 0
    for size, p_ref, q_ref in zip(sizes, mine, theirs):
        for i in range(size):
            j, k = place % depth, place // depth
            chip = (own // 2) ^ (j * width + k)
            p, q = p_ref[i], q_ref[i]
            before, after = jnp.where(c == 0, p, q), jnp.where(c == 0, q, p)
            packed[pl.ds(pl.multiple_of(chip * 2 * rows, 2 * rows), 2 * rows), :] = (
                jnp.concatenate([before, after], 0)
            )
            place += 1
    ids = lax.broadcasted_iota(jnp.int32, placement.shape, 1)
    total = None
    for slot, weight in ((own, down), (own ^ 1, core_down)):
        full = lax.dot_general(
            packed[...], weight[...], (((1,), (1,)), ((), ())), preferred_element_type=jnp.float32
        )
        owner = jnp.sum(jnp.where(placement[...] == slot, ids, 0), axis=1, keepdims=True)
        chosen = across(jnp.where(index[...] == owner, 1, 0))[:, : full.shape[1]]
        total = jnp.where(chosen == 1, full, 0.0 if total is None else total)
    low[...] = total.astype(low.dtype)


def collect(placement, index, downs, mine, theirs, depth, width):
    sizes = [v.shape[0] for v in mine]
    rows, model = mine[0].shape[1:]
    requests = 2 * depth * width * rows
    return pl.pallas_call(
        functools.partial(collect_kernel, depth, width, sizes),
        out_shape=[
            pltpu.VMEM((requests, model), jnp.bfloat16),
            jax.ShapeDtypeStruct((requests, downs[0].shape[0]), jnp.bfloat16),
        ],
        in_specs=[NEAR] * (4 + 2 * len(sizes)),
        out_specs=[NEAR] * 2,
        cost_estimate=pl.CostEstimate(
            flops=4 * requests * model * 64, bytes_accessed=1 << 20, transcendentals=0
        ),
        compiler_params=pltpu.CompilerParams(vmem_limit_bytes=2 << 20),
        name="collect",
    )(placement, index, *downs, *[near(v) for v in mine], *[near(v) for v in theirs])


def add_kernel(*refs):
    total = refs[0][...]
    for ref in refs[1:-1]:
        total = total + ref[...]
    refs[-1][...] = total


def add(*values):
    return pl.pallas_call(
        add_kernel,
        out_shape=jax.ShapeDtypeStruct(values[0].shape, values[0].dtype),
        in_specs=[NEAR] * len(values),
        out_specs=NEAR,
        cost_estimate=pl.CostEstimate(flops=0, bytes_accessed=1 << 14, transcendentals=0),
        compiler_params=pltpu.CompilerParams(vmem_limit_bytes=1 << 20),
        name="add",
    )(*values)


def multiply_kernel(start, n, begun, firsts, *refs):
    tokens, refs = refs[1], refs[2:]
    pieces, refs = refs[:n], refs[n:]
    before, refs = refs[:begun], refs[begun:]
    sources, (out, *targets) = refs[: len(firsts)], refs[len(firsts) :]
    copies = copies_of(sources, firsts, targets[:-1], targets[-1]) if firsts else []
    for copy in copies:
        copy.start()

    def tile(here):
        total = piecewise(tokens, pieces, start, here)
        if begun:
            total = total + before[0][:, here]
        out[:, here] = total

    for_columns(out.shape[1], tile)
    for copy in copies:
        copy.wait()


def multiply(after, tokens, pieces, start, begun, fetched, rows, name):
    requests = tokens.shape[0]
    hidden = pieces[0].shape[1]
    n = len(fetched)
    operands = [after, near(tokens)] + [near(p) for p in pieces] + [near(b) for b in begun]
    in_specs = [FAR] + [NEAR] * (len(operands) - 1) + [STORED] * n
    operands += [far(source) for source, first in fetched]
    return pl.pallas_call(
        functools.partial(
            multiply_kernel, start, len(pieces), len(begun), [first for source, first in fetched]
        ),
        out_shape=[pltpu.VMEM((requests, hidden), jnp.float32)]
        + [pltpu.VMEM((rows, hidden), tokens.dtype)] * n,
        in_specs=in_specs,
        out_specs=[NEAR] * (1 + n),
        scratch_shapes=[pltpu.SemaphoreType.DMA((n,))] if n else [],
        cost_estimate=pl.CostEstimate(
            flops=2 * requests * sum(p.shape[0] for p in pieces) * hidden,
            bytes_accessed=16 << 20,
            transcendentals=0,
        ),
        compiler_params=pltpu.CompilerParams(vmem_limit_bytes=2 << 20),
        name=name,
    )(*operands)


def finish_kernel(start, n, m, index, tokens, adapter_up, gate_pre, up_pre, *refs):
    pieces, refs = refs[:n], refs[n:]
    lows, (out, expanded) = refs[:m], refs[m:]
    rank = lows[0].shape[1]
    mixed = lows[0][...]
    for low in lows[1:]:
        mixed = mixed + low[...]
    group = TILE // rank
    lane = lax.broadcasted_iota(jnp.int32, (rank, TILE), 1)
    repeat = (lane % rank == lax.broadcasted_iota(jnp.int32, (rank, TILE), 0)).astype(jnp.bfloat16)
    wide = jnp.dot(mixed, repeat, preferred_element_type=jnp.float32)
    of_lane = lax.broadcasted_iota(jnp.int32, (mixed.shape[0], TILE), 1) // rank
    relative = jnp.concatenate([across(index[...])] * (TILE // mixed.shape[0]), 1) - of_lane
    for i in range(expanded.shape[1] // TILE):
        expanded[:, i * TILE : (i + 1) * TILE] = jnp.where(
            relative == i * group, wide, 0.0
        ).astype(jnp.bfloat16)

    width = out.shape[1]
    for first in range(0, width, WIDE):
        here = pl.ds(first, min(WIDE, width - first))
        up = up_pre[:, here] + piecewise(tokens, pieces, start, here)
        up = up + jnp.dot(expanded[...], adapter_up[:, here], preferred_element_type=jnp.float32)
        gate = gate_pre[:, here]
        out[:, here] = (gate / (1.0 + jnp.exp(-gate)) * up).astype(out.dtype)


def finish(index, tokens, adapter_up, gate_pre, up_pre, pieces, start, lows):
    requests, hidden = gate_pre.shape
    return pl.pallas_call(
        functools.partial(finish_kernel, start, len(pieces), len(lows)),
        out_shape=jax.ShapeDtypeStruct((requests, hidden), jnp.bfloat16),
        in_specs=[NEAR] * (5 + len(pieces) + len(lows)),
        out_specs=NEAR,
        scratch_shapes=[pltpu.VMEM((requests, adapter_up.shape[0]), jnp.bfloat16)],
        cost_estimate=pl.CostEstimate(
            flops=2 * requests * (adapter_up.shape[0] + sum(p.shape[0] for p in pieces)) * hidden,
            bytes_accessed=4 << 20,
            transcendentals=requests * hidden,
        ),
        compiler_params=pltpu.CompilerParams(vmem_limit_bytes=3 << 20),
        name="finish",
    )(
        index,
        near(tokens),
        near(adapter_up),
        near(gate_pre),
        near(up_pre),
        *[near(p) for p in pieces],
        *lows,
    )


def on_chip(tokens, gate_weight, up_weight, down, up, request_adapter_index, placement):
    depth, width = plan(lax.axis_size("tensor"))
    model, hidden = gate_weight.shape
    index = request_adapter_index[None, :]
    unit = model // PIECES
    firsts = [i * unit for i in range(PIECES)]
    up = up.reshape(-1, hidden)
    down = jnp.swapaxes(down[0], 0, 1)
    own = tokens[None]
    core, column, line_1, line_2 = 1, 2, 2 * width, 4 * width

    block_2 = swap(own, line_2)
    block_1 = swap(own, line_1)
    column_0 = swap(own, column)
    core_down = swap(down, core)
    gates = fetch([(gate_weight, first) for first in firsts[:5]], unit, "fetch_0")
    block_2 = tie(block_2, gates[:1])
    block_3 = swap(block_2, line_1)
    blocks_12 = pack([block_1, block_2], [gates[0], column_0, core_down])
    columns_12 = swap(blocks_12, column)
    gates += fetch([(gate_weight, first) for first in firsts[5:7]], unit, "fetch_1", [blocks_12])
    block_3 = tie(block_3, gates[5:6])
    column_3 = swap(block_3, column)
    line = pack([own, blocks_12, block_3], [])
    core_line = swap(line, core)
    more = [(gate_weight, firsts[7]), (up_weight, firsts[0]), (up_weight, firsts[1])]
    last_gate, up_0, up_1 = fetch(more, unit, "fetch_2", [line])
    gates.append(last_gate)
    columns = pack([column_0, columns_12, column_3], [up_0])
    core_columns = swap(columns, core)
    packed, low = collect(
        placement[None, :],
        index,
        [down, core_down],
        [line, columns],
        [core_line, core_columns],
        depth,
        width,
    )

    low_1 = add(low, swap(low, line_2))
    gate_pre, *ups = multiply(
        low,
        packed,
        gates[:4],
        0,
        [],
        [(up_weight, first) for first in firsts[2:4]],
        unit,
        "gate_a",
    )
    ups = [up_0, up_1] + ups
    low_2 = add(low_1, swap(low_1, line_1))
    gate_pre, *more_ups = multiply(
        low_1,
        packed,
        gates[4:],
        firsts[4],
        [gate_pre],
        [(up_weight, first) for first in firsts[4:7]],
        unit,
        "gate_b",
    )
    lows = [low_2, swap(low_2, column)]
    up_pre, near_up, last_up = multiply(
        low_2, packed, ups, 0, [], [(up, 0), (up_weight, firsts[7])], unit, "up_a"
    )
    return finish(
        index, packed, near_up, gate_pre, up_pre, more_ups + [last_up], firsts[4], lows
    )


def streamed(
    tokens,
    gate_weight,
    up_weight,
    adapter_down_weight,
    adapter_up_weight,
    request_adapter_index,
    adapter_request_lists,
    placement,
):
    count = lax.axis_size("tensor")
    depth, width = plan(count)
    rows = tokens.shape[0]
    requests = request_adapter_index.shape[0]
    adapters = placement.shape[0]
    rank_width = adapter_down_weight.shape[2]
    own = lax.axis_index("tensor")

    by_line = [tokens] + [send(tokens, j, 0, 0) for j in range(1, depth)]
    plane = list(by_line)
    for k in range(1, width):
        plane += [send(block, 0, k, 0) for block in by_line]
    half = jnp.concatenate(plane, 0)
    other = send(half, 0, 0, 1)
    gathered = jnp.concatenate([half, other], 0)

    slot = jnp.arange(requests, dtype=jnp.int32)
    block, inner = slot // rows, slot % rows
    j, k, m = block % depth, block // depth % width, block // (depth * width)
    origin = ((own // (2 * width) - j) % depth * width + (own // 2 - k) % width) * 2 + (own + m) % 2
    row_id = origin * rows + inner

    owner = jnp.sum(jnp.where(placement == own, jnp.arange(adapters, dtype=jnp.int32), 0))
    wanted = lax.dynamic_slice_in_dim(adapter_request_lists, owner, 1, 0)[0]
    picker = (wanted[:, None] == row_id[None, :]).astype(jnp.bfloat16)
    picked = jnp.dot(picker, gathered, preferred_element_type=jnp.float32).astype(jnp.bfloat16)
    low_rank = jnp.dot(picked, adapter_down_weight[0], preferred_element_type=jnp.float32)
    spread = (jnp.arange(requests, dtype=jnp.int32)[:, None] == wanted[None, :]).astype(jnp.bfloat16)
    mixed = jnp.dot(spread, low_rank.astype(jnp.bfloat16), preferred_element_type=jnp.float32)
    mixed = mixed.astype(jnp.bfloat16)
    step = 1
    while step < count:
        mixed = mixed + lax.ppermute(mixed, "tensor", [(i, i ^ step) for i in range(count)])
        step *= 2

    gate_pre = jnp.dot(gathered, gate_weight, preferred_element_type=jnp.float32)
    up_pre = jnp.dot(gathered, up_weight, preferred_element_type=jnp.float32)
    here = (row_id[:, None] == jnp.arange(requests, dtype=jnp.int32)[None, :]).astype(jnp.bfloat16)
    mine = jnp.dot(here, mixed, preferred_element_type=jnp.float32).astype(jnp.bfloat16)
    index = jnp.take(request_adapter_index, row_id)
    chosen = index[:, None] == jnp.arange(adapters, dtype=jnp.int32)[None, :]
    expanded = jnp.where(chosen[:, :, None], mine[:, None, :], jnp.zeros((), jnp.bfloat16))
    delta = jnp.dot(
        expanded.reshape(requests, adapters * rank_width),
        adapter_up_weight.reshape(adapters * rank_width, -1),
        preferred_element_type=jnp.float32,
    )
    hidden = (jax.nn.silu(gate_pre) * (up_pre + delta)).astype(jnp.bfloat16)
    return jnp.dot(here.T, hidden, preferred_element_type=jnp.float32).astype(jnp.bfloat16)


def body(
    tokens,
    gate_weight,
    up_weight,
    adapter_down_weight,
    adapter_up_weight,
    request_adapter_index,
    adapter_request_lists,
    placement,
):
    count = lax.axis_size("tensor")
    if plan(count) == (4, 2) and tokens.shape[0] == 8:
        return on_chip(
            tokens,
            gate_weight,
            up_weight,
            adapter_down_weight,
            adapter_up_weight,
            request_adapter_index,
            placement,
        )
    return streamed(
        tokens,
        gate_weight,
        up_weight,
        adapter_down_weight,
        adapter_up_weight,
        request_adapter_index,
        adapter_request_lists,
        placement,
    )


def solution(mesh):
    in_specs = (
        P(("groups", "tensor"), None),
        P(None, "tensor"),
        P(None, "tensor"),
        P(("groups", "tensor"), None, None),
        P("groups", None, "tensor"),
        P("groups"),
        P("groups", None),
        P("groups"),
    )
    out_specs = P("groups", "tensor")
    return jax.shard_map(body, mesh=mesh, in_specs=in_specs, out_specs=out_specs, check_vma=False)
```

```python
import functools

import jax
import jax.numpy as jnp
from jax import lax
from jax.experimental import pallas as pl
from jax.experimental.pallas import tpu as pltpu
from jax.sharding import PartitionSpec as P

TILE = 256
WIDE = 512
PIECES = 8
NEAR = pl.BlockSpec(memory_space=pltpu.VMEM)
FAR = pl.BlockSpec(memory_space=pl.ANY)
STORED = pl.BlockSpec(memory_space=pltpu.HBM)


def near(value):
    return pltpu.with_memory_space_constraint(value, pltpu.VMEM)


def far(value):
    return pltpu.with_memory_space_constraint(value, pltpu.HBM)


def plan(count):
    lines = 1
    while lines * lines < count // 2:
        lines *= 2
    return lines, count // 2 // lines


def send(value, da, db, dc):
    count = lax.axis_size("tensor")
    depth, width = plan(count)
    pairs = []
    for i in range(count):
        a, b, c = i // (2 * width), i // 2 % width, i % 2
        pairs.append((i, ((a + da) % depth * width + (b + db) % width) * 2 + (c + dc) % 2))
    return lax.ppermute(value, "tensor", pairs)


def swap(value, mask):
    pairs = [(i, i ^ mask) for i in range(lax.axis_size("tensor"))]
    return lax.ppermute(value, "tensor", pairs)


def copies_of(sources, firsts, targets, sems):
    return [
        pltpu.make_async_copy(source.at[pl.ds(first, target.shape[0])], target, sems.at[i])
        for i, (source, first, target) in enumerate(zip(sources, firsts, targets))
    ]


def fetch_kernel(firsts, joined, skipped, *refs):
    n = len(firsts)
    sources, parts, refs = refs[:n], refs[n : n + joined], refs[n + joined + skipped :]
    targets, sems = refs[:n], refs[-1]
    copies = copies_of(sources, firsts, targets, sems)
    for copy in copies:
        copy.start()
    row = 0
    for part in parts:
        rows = part.shape[0]
        refs[n][row : row + rows, :] = part[...]
        row += rows
    for copy in copies:
        copy.wait()


def fetch(fetched, rows, name, after=(), join=()):
    n = len(fetched)
    width = fetched[0][0].shape[1]
    out_shape = [pltpu.VMEM((rows, width), fetched[0][0].dtype)] * n
    if join:
        out_shape.append(
            pltpu.VMEM((sum(v.shape[0] for v in join), join[0].shape[1]), join[0].dtype)
        )
    arrived = pl.pallas_call(
        functools.partial(
            fetch_kernel, [first for source, first in fetched], len(join), len(after)
        ),
        out_shape=out_shape,
        in_specs=[STORED] * n + [NEAR] * len(join) + [FAR] * len(after),
        out_specs=[NEAR] * len(out_shape),
        scratch_shapes=[pltpu.SemaphoreType.DMA((n,))],
        cost_estimate=pl.CostEstimate(
            flops=0, bytes_accessed=n * rows * width * 2, transcendentals=0
        ),
        compiler_params=pltpu.CompilerParams(vmem_limit_bytes=3 << 20 if join else 1 << 20),
        name=name,
    )(*[far(source) for source, first in fetched], *[near(v) for v in join], *after)
    return list(arrived)


def across(row):
    n = row.shape[1]
    return jnp.broadcast_to(row, (n, n)).T


def pack_kernel(n, *refs):
    place = 0
    for ref in refs[:n]:
        for i in range(ref.shape[0]):
            refs[-1][place] = ref[i]
            place += 1


def pack(blocks, after):
    rows, model = blocks[0].shape[1:]
    n = len(blocks)
    return pl.pallas_call(
        functools.partial(pack_kernel, n),
        out_shape=pltpu.VMEM((sum(b.shape[0] for b in blocks), rows, model), jnp.bfloat16),
        in_specs=[NEAR] * n + [FAR] * len(after),
        out_specs=NEAR,
        cost_estimate=pl.CostEstimate(flops=0, bytes_accessed=1 << 18, transcendentals=0),
        compiler_params=pltpu.CompilerParams(vmem_limit_bytes=1 << 20),
        name="pack",
    )(*[near(v) for v in blocks], *after)


def tie_kernel(*refs):
    pass


def tie(value, after):
    return pl.pallas_call(
        tie_kernel,
        out_shape=jax.ShapeDtypeStruct(value.shape, value.dtype),
        in_specs=[FAR] * (1 + len(after)),
        out_specs=FAR,
        input_output_aliases={0: 0},
        cost_estimate=pl.CostEstimate(flops=0, bytes_accessed=1 << 10, transcendentals=0),
        compiler_params=pltpu.CompilerParams(vmem_limit_bytes=1 << 20),
        name="tie",
    )(value, *after)


def piecewise(tokens, pieces, start, here):
    total = None
    for piece in pieces:
        rows = piece.shape[0]
        term = jnp.dot(
            tokens[:, start : start + rows], piece[:, here], preferred_element_type=jnp.float32
        )
        total = term if total is None else total + term
        start += rows
    return total


def for_columns(width, tile):
    @pl.loop(0, width // WIDE)
    def _(i):
        tile(pl.ds(pl.multiple_of(i * WIDE, WIDE), WIDE))

    if width % WIDE:
        tile(pl.ds(width // WIDE * WIDE, width % WIDE))


def collect_kernel(depth, width, sizes, placement, index, downs, *refs):
    mine, theirs = refs[: len(sizes)], refs[len(sizes) : 2 * len(sizes)]
    packed, low = refs[2 * len(sizes) :]
    own = lax.axis_index("tensor")
    c = own % 2
    rows = packed.shape[0] // (2 * depth * width)
    place = 0
    for size, p_ref, q_ref in zip(sizes, mine, theirs):
        for i in range(size):
            j, k = place % depth, place // depth
            chip = (own // 2) ^ (j * width + k)
            p, q = p_ref[i], q_ref[i]
            before, after = jnp.where(c == 0, p, q), jnp.where(c == 0, q, p)
            packed[pl.ds(pl.multiple_of(chip * 2 * rows, 2 * rows), 2 * rows), :] = (
                jnp.concatenate([before, after], 0)
            )
            place += 1
    full = lax.dot_general(
        packed[...], downs[...], (((1,), (1,)), ((), ())), preferred_element_type=jnp.float32
    )
    rank = low.shape[1]
    ids = lax.broadcasted_iota(jnp.int32, placement.shape, 1)
    owners = [
        jnp.sum(jnp.where(placement[...] == slot, ids, 0), axis=1, keepdims=True)
        for slot in (own, own ^ 1)
    ]
    adapter = across(index[...])[:, :rank]
    kept = jnp.where(adapter == owners[0], full[:, :rank], 0.0)
    low[...] = jnp.where(adapter == owners[1], full[:, rank:], kept).astype(low.dtype)


def collect(placement, index, downs, mine, theirs, depth, width):
    sizes = [v.shape[0] for v in mine]
    rows, model = mine[0].shape[1:]
    requests = 2 * depth * width * rows
    return pl.pallas_call(
        functools.partial(collect_kernel, depth, width, sizes),
        out_shape=[
            pltpu.VMEM((requests, model), jnp.bfloat16),
            jax.ShapeDtypeStruct((requests, downs.shape[0] // 2), jnp.bfloat16),
        ],
        in_specs=[NEAR] * (3 + 2 * len(sizes)),
        out_specs=[NEAR] * 2,
        cost_estimate=pl.CostEstimate(
            flops=4 * requests * model * 64, bytes_accessed=1 << 20, transcendentals=0
        ),
        compiler_params=pltpu.CompilerParams(vmem_limit_bytes=2 << 20),
        name="collect",
    )(placement, index, near(downs), *[near(v) for v in mine], *[near(v) for v in theirs])


def add_kernel(*refs):
    total = refs[0][...]
    for ref in refs[1:-1]:
        total = total + ref[...]
    refs[-1][...] = total


def add(*values):
    return pl.pallas_call(
        add_kernel,
        out_shape=jax.ShapeDtypeStruct(values[0].shape, values[0].dtype),
        in_specs=[NEAR] * len(values),
        out_specs=NEAR,
        cost_estimate=pl.CostEstimate(flops=0, bytes_accessed=1 << 14, transcendentals=0),
        compiler_params=pltpu.CompilerParams(vmem_limit_bytes=1 << 20),
        name="add",
    )(*values)


def multiply_kernel(start, n, begun, firsts, gating, *refs):
    tokens, refs = refs[1], refs[2:]
    pieces, refs = refs[:n], refs[n:]
    before, refs = refs[:begun], refs[begun:]
    sources, (out, *targets) = refs[: len(firsts)], refs[len(firsts) :]
    copies = copies_of(sources, firsts, targets[:-1], targets[-1]) if firsts else []
    for copy in copies:
        copy.start()

    def tile(here):
        total = piecewise(tokens, pieces, start, here)
        if begun:
            total = total + before[0][:, here]
        out[:, here] = total / (1.0 + jnp.exp(-total)) if gating else total

    for_columns(out.shape[1], tile)
    for copy in copies:
        copy.wait()


def multiply(after, tokens, pieces, start, begun, fetched, rows, name, gating=False):
    requests = tokens.shape[0]
    hidden = pieces[0].shape[1]
    n = len(fetched)
    operands = [after, near(tokens)] + [near(p) for p in pieces] + [near(b) for b in begun]
    in_specs = [FAR] + [NEAR] * (len(operands) - 1) + [STORED] * n
    operands += [far(source) for source, first in fetched]
    return pl.pallas_call(
        functools.partial(
            multiply_kernel,
            start,
            len(pieces),
            len(begun),
            [first for source, first in fetched],
            gating,
        ),
        out_shape=[pltpu.VMEM((requests, hidden), jnp.float32)]
        + [pltpu.VMEM((rows, hidden), tokens.dtype)] * n,
        in_specs=in_specs,
        out_specs=[NEAR] * (1 + n),
        scratch_shapes=[pltpu.SemaphoreType.DMA((n,))] if n else [],
        cost_estimate=pl.CostEstimate(
            flops=2 * requests * sum(p.shape[0] for p in pieces) * hidden,
            bytes_accessed=16 << 20,
            transcendentals=0,
        ),
        compiler_params=pltpu.CompilerParams(vmem_limit_bytes=2 << 20),
        name=name,
    )(*operands)


def finish_kernel(start, n, m, index, tokens, adapter_up, gate, up_pre, *refs):
    pieces, refs = refs[:n], refs[n:]
    lows, (stored, expanded, out, sems) = refs[:m], refs[m:]
    rank = lows[0].shape[1]
    mixed = lows[0][...]
    for low in lows[1:]:
        mixed = mixed + low[...]
    group = TILE // rank
    lane = lax.broadcasted_iota(jnp.int32, (rank, TILE), 1)
    repeat = (lane % rank == lax.broadcasted_iota(jnp.int32, (rank, TILE), 0)).astype(jnp.bfloat16)
    wide = jnp.dot(mixed, repeat, preferred_element_type=jnp.float32)
    of_lane = lax.broadcasted_iota(jnp.int32, (mixed.shape[0], TILE), 1) // rank
    relative = jnp.concatenate([across(index[...])] * (TILE // mixed.shape[0]), 1) - of_lane
    for i in range(expanded.shape[1] // TILE):
        expanded[:, i * TILE : (i + 1) * TILE] = jnp.where(
            relative == i * group, wide, 0.0
        ).astype(jnp.bfloat16)

    width = out.shape[1]
    copies = []
    for first in range(0, width, WIDE):
        here = pl.ds(first, min(WIDE, width - first))
        up = up_pre[:, here] + piecewise(tokens, pieces, start, here)
        up = up + jnp.dot(expanded[...], adapter_up[:, here], preferred_element_type=jnp.float32)
        out[:, here] = (gate[:, here] * up).astype(out.dtype)
        copies.append(
            pltpu.make_async_copy(out.at[:, here], stored.at[:, here], sems.at[len(copies)])
        )
        copies[-1].start()
    for copy in copies:
        copy.wait()


def finish(index, tokens, adapter_up, gate, up_pre, pieces, start, lows):
    requests, hidden = gate.shape
    return pl.pallas_call(
        functools.partial(finish_kernel, start, len(pieces), len(lows)),
        out_shape=jax.ShapeDtypeStruct((requests, hidden), jnp.bfloat16),
        in_specs=[NEAR] * (5 + len(pieces) + len(lows)),
        out_specs=STORED,
        scratch_shapes=[
            pltpu.VMEM((requests, adapter_up.shape[0]), jnp.bfloat16),
            pltpu.VMEM((requests, hidden), jnp.bfloat16),
            pltpu.SemaphoreType.DMA((-(-hidden // WIDE),)),
        ],
        cost_estimate=pl.CostEstimate(
            flops=2 * requests * (adapter_up.shape[0] + sum(p.shape[0] for p in pieces)) * hidden,
            bytes_accessed=4 << 20,
            transcendentals=requests * hidden,
        ),
        compiler_params=pltpu.CompilerParams(vmem_limit_bytes=3 << 20),
        name="finish",
    )(
        index,
        near(tokens),
        near(adapter_up),
        near(gate),
        near(up_pre),
        *[near(p) for p in pieces],
        *lows,
    )


def on_chip(tokens, gate_weight, up_weight, down, up, request_adapter_index, placement):
    depth, width = plan(lax.axis_size("tensor"))
    model, hidden = gate_weight.shape
    index = request_adapter_index[None, :]
    unit = model // PIECES
    firsts = [i * unit for i in range(PIECES)]
    up = up.reshape(-1, hidden)
    down = jnp.swapaxes(down[0], 0, 1)
    own = tokens[None]
    core, column, line_1, line_2 = 1, 2, 2 * width, 4 * width

    block_2 = swap(own, line_2)
    block_1 = swap(own, line_1)
    column_0 = swap(own, column)
    core_down = swap(down, core)
    gates = fetch([(gate_weight, first) for first in firsts[:5]], unit, "fetch_0")
    block_2 = tie(block_2, gates[:1])
    block_3 = swap(block_2, line_1)
    blocks_12 = pack([block_1, block_2], [gates[0], column_0, core_down])
    columns_12 = swap(blocks_12, column)
    *more_gates, downs = fetch(
        [(gate_weight, first) for first in firsts[5:7]],
        unit,
        "fetch_1",
        [blocks_12],
        [down, core_down],
    )
    gates += more_gates
    block_3 = tie(block_3, gates[5:6])
    column_3 = swap(block_3, column)
    line = pack([own, blocks_12, block_3], [])
    core_line = swap(line, core)
    last_gate, *ups = fetch(
        [(gate_weight, firsts[7])] + [(up_weight, first) for first in firsts[:3]],
        unit,
        "fetch_2",
        [line],
    )
    gates.append(last_gate)
    columns = pack([column_0, columns_12, column_3], ups[:1])
    core_columns = swap(columns, core)
    packed, low = collect(
        placement[None, :],
        index,
        downs,
        [line, columns],
        [core_line, core_columns],
        depth,
        width,
    )

    low_1 = add(low, swap(low, line_2))
    gate, *more_ups = multiply(
        low,
        packed,
        gates[:4],
        0,
        [],
        [(up_weight, first) for first in firsts[3:5]],
        unit,
        "gate_a",
    )
    ups += more_ups
    low_2 = add(low_1, swap(low_1, line_1))
    gate, *more_ups = multiply(
        low_1,
        packed,
        gates[4:],
        firsts[4],
        [gate],
        [(up_weight, first) for first in firsts[5:7]],
        unit,
        "gate_b",
        gating=True,
    )
    ups += more_ups
    lows = [low_2, swap(low_2, column)]
    up_pre, near_up, last_up = multiply(
        low_2, packed, ups[:4], 0, [], [(up, 0), (up_weight, firsts[7])], unit, "up_a"
    )
    ups.append(last_up)
    return finish(index, packed, near_up, gate, up_pre, ups[4:], firsts[4], lows)


def streamed(
    tokens,
    gate_weight,
    up_weight,
    adapter_down_weight,
    adapter_up_weight,
    request_adapter_index,
    adapter_request_lists,
    placement,
):
    count = lax.axis_size("tensor")
    depth, width = plan(count)
    rows = tokens.shape[0]
    requests = request_adapter_index.shape[0]
    adapters = placement.shape[0]
    rank_width = adapter_down_weight.shape[2]
    own = lax.axis_index("tensor")

    by_line = [tokens] + [send(tokens, j, 0, 0) for j in range(1, depth)]
    plane = list(by_line)
    for k in range(1, width):
        plane += [send(block, 0, k, 0) for block in by_line]
    half = jnp.concatenate(plane, 0)
    other = send(half, 0, 0, 1)
    gathered = jnp.concatenate([half, other], 0)

    slot = jnp.arange(requests, dtype=jnp.int32)
    block, inner = slot // rows, slot % rows
    j, k, m = block % depth, block // depth % width, block // (depth * width)
    origin = ((own // (2 * width) - j) % depth * width + (own // 2 - k) % width) * 2 + (own + m) % 2
    row_id = origin * rows + inner

    owner = jnp.sum(jnp.where(placement == own, jnp.arange(adapters, dtype=jnp.int32), 0))
    wanted = lax.dynamic_slice_in_dim(adapter_request_lists, owner, 1, 0)[0]
    picker = (wanted[:, None] == row_id[None, :]).astype(jnp.bfloat16)
    picked = jnp.dot(picker, gathered, preferred_element_type=jnp.float32).astype(jnp.bfloat16)
    low_rank = jnp.dot(picked, adapter_down_weight[0], preferred_element_type=jnp.float32)
    spread = (jnp.arange(requests, dtype=jnp.int32)[:, None] == wanted[None, :]).astype(jnp.bfloat16)
    mixed = jnp.dot(spread, low_rank.astype(jnp.bfloat16), preferred_element_type=jnp.float32)
    mixed = mixed.astype(jnp.bfloat16)
    step = 1
    while step < count:
        mixed = mixed + lax.ppermute(mixed, "tensor", [(i, i ^ step) for i in range(count)])
        step *= 2

    gate_pre = jnp.dot(gathered, gate_weight, preferred_element_type=jnp.float32)
    up_pre = jnp.dot(gathered, up_weight, preferred_element_type=jnp.float32)
    here = (row_id[:, None] == jnp.arange(requests, dtype=jnp.int32)[None, :]).astype(jnp.bfloat16)
    mine = jnp.dot(here, mixed, preferred_element_type=jnp.float32).astype(jnp.bfloat16)
    index = jnp.take(request_adapter_index, row_id)
    chosen = index[:, None] == jnp.arange(adapters, dtype=jnp.int32)[None, :]
    expanded = jnp.where(chosen[:, :, None], mine[:, None, :], jnp.zeros((), jnp.bfloat16))
    delta = jnp.dot(
        expanded.reshape(requests, adapters * rank_width),
        adapter_up_weight.reshape(adapters * rank_width, -1),
        preferred_element_type=jnp.float32,
    )
    hidden = (jax.nn.silu(gate_pre) * (up_pre + delta)).astype(jnp.bfloat16)
    return jnp.dot(here.T, hidden, preferred_element_type=jnp.float32).astype(jnp.bfloat16)


def body(
    tokens,
    gate_weight,
    up_weight,
    adapter_down_weight,
    adapter_up_weight,
    request_adapter_index,
    adapter_request_lists,
    placement,
):
    count = lax.axis_size("tensor")
    if plan(count) == (4, 2) and tokens.shape[0] == 8:
        return on_chip(
            tokens,
            gate_weight,
            up_weight,
            adapter_down_weight,
            adapter_up_weight,
            request_adapter_index,
            placement,
        )
    return streamed(
        tokens,
        gate_weight,
        up_weight,
        adapter_down_weight,
        adapter_up_weight,
        request_adapter_index,
        adapter_request_lists,
        placement,
    )


def solution(mesh):
    in_specs = (
        P(("groups", "tensor"), None),
        P(None, "tensor"),
        P(None, "tensor"),
        P(("groups", "tensor"), None, None),
        P("groups", None, "tensor"),
        P("groups"),
        P("groups", None),
        P("groups"),
    )
    out_specs = P("groups", "tensor")
    return jax.shard_map(body, mesh=mesh, in_specs=in_specs, out_specs=out_specs, check_vma=False)
```

```python
import functools

import jax
import jax.numpy as jnp
from jax import lax
from jax.experimental import pallas as pl
from jax.experimental.pallas import tpu as pltpu
from jax.sharding import PartitionSpec as P

TILE = 256
WIDE = 512
PIECES = 8
NEAR = pl.BlockSpec(memory_space=pltpu.VMEM)
FAR = pl.BlockSpec(memory_space=pl.ANY)
STORED = pl.BlockSpec(memory_space=pltpu.HBM)


def near(value):
    return pltpu.with_memory_space_constraint(value, pltpu.VMEM)


def far(value):
    return pltpu.with_memory_space_constraint(value, pltpu.HBM)


def plan(count):
    lines = 1
    while lines * lines < count // 2:
        lines *= 2
    return lines, count // 2 // lines


def send(value, da, db, dc):
    count = lax.axis_size("tensor")
    depth, width = plan(count)
    pairs = []
    for i in range(count):
        a, b, c = i // (2 * width), i // 2 % width, i % 2
        pairs.append((i, ((a + da) % depth * width + (b + db) % width) * 2 + (c + dc) % 2))
    return lax.ppermute(value, "tensor", pairs)


def swap(value, mask):
    pairs = [(i, i ^ mask) for i in range(lax.axis_size("tensor"))]
    return lax.ppermute(value, "tensor", pairs)


def copies_of(sources, firsts, targets, sems):
    return [
        pltpu.make_async_copy(source.at[pl.ds(first, target.shape[0])], target, sems.at[i])
        for i, (source, first, target) in enumerate(zip(sources, firsts, targets))
    ]


def fetch_kernel(firsts, joined, skipped, *refs):
    n = len(firsts)
    sources, parts, refs = refs[:n], refs[n : n + joined], refs[n + joined + skipped :]
    targets, sems = refs[:n], refs[-1]
    copies = copies_of(sources, firsts, targets, sems)
    for copy in copies:
        copy.start()
    row = 0
    for part in parts:
        rows = part.shape[0]
        refs[n][row : row + rows, :] = part[...]
        row += rows
    for copy in copies:
        copy.wait()


def fetch(fetched, rows, name, after=(), join=()):
    n = len(fetched)
    width = fetched[0][0].shape[1]
    out_shape = [pltpu.VMEM((rows, width), fetched[0][0].dtype)] * n
    if join:
        out_shape.append(
            pltpu.VMEM((sum(v.shape[0] for v in join), join[0].shape[1]), join[0].dtype)
        )
    arrived = pl.pallas_call(
        functools.partial(
            fetch_kernel, [first for source, first in fetched], len(join), len(after)
        ),
        out_shape=out_shape,
        in_specs=[STORED] * n + [NEAR] * len(join) + [FAR] * len(after),
        out_specs=[NEAR] * len(out_shape),
        scratch_shapes=[pltpu.SemaphoreType.DMA((n,))],
        cost_estimate=pl.CostEstimate(
            flops=0, bytes_accessed=n * rows * width * 2, transcendentals=0
        ),
        compiler_params=pltpu.CompilerParams(vmem_limit_bytes=3 << 20 if join else 1 << 20),
        name=name,
    )(*[far(source) for source, first in fetched], *[near(v) for v in join], *after)
    return list(arrived)


def across(row):
    n = row.shape[1]
    return jnp.broadcast_to(row, (n, n)).T


def pack_kernel(n, *refs):
    place = 0
    for ref in refs[:n]:
        for i in range(ref.shape[0]):
            refs[-1][place] = ref[i]
            place += 1


def pack(blocks, after):
    rows, model = blocks[0].shape[1:]
    n = len(blocks)
    return pl.pallas_call(
        functools.partial(pack_kernel, n),
        out_shape=pltpu.VMEM((sum(b.shape[0] for b in blocks), rows, model), jnp.bfloat16),
        in_specs=[NEAR] * n + [FAR] * len(after),
        out_specs=NEAR,
        cost_estimate=pl.CostEstimate(flops=0, bytes_accessed=1 << 18, transcendentals=0),
        compiler_params=pltpu.CompilerParams(vmem_limit_bytes=1 << 20),
        name="pack",
    )(*[near(v) for v in blocks], *after)


def tie_kernel(*refs):
    pass


def tie(value, after):
    return pl.pallas_call(
        tie_kernel,
        out_shape=jax.ShapeDtypeStruct(value.shape, value.dtype),
        in_specs=[FAR] * (1 + len(after)),
        out_specs=FAR,
        input_output_aliases={0: 0},
        cost_estimate=pl.CostEstimate(flops=0, bytes_accessed=1 << 10, transcendentals=0),
        compiler_params=pltpu.CompilerParams(vmem_limit_bytes=1 << 20),
        name="tie",
    )(value, *after)


def piecewise(tokens, pieces, start, here):
    total = None
    for piece in pieces:
        rows = piece.shape[0]
        term = jnp.dot(
            tokens[:, start : start + rows], piece[:, here], preferred_element_type=jnp.float32
        )
        total = term if total is None else total + term
        start += rows
    return total


def for_columns(width, tile):
    @pl.loop(0, width // WIDE)
    def _(i):
        tile(pl.ds(pl.multiple_of(i * WIDE, WIDE), WIDE))

    if width % WIDE:
        tile(pl.ds(width // WIDE * WIDE, width % WIDE))


def collect_kernel(depth, width, sizes, placement, index, downs, *refs):
    mine, theirs = refs[: len(sizes)], refs[len(sizes) : 2 * len(sizes)]
    packed, low = refs[2 * len(sizes) :]
    own = lax.axis_index("tensor")
    c = own % 2
    rows = packed.shape[0] // (2 * depth * width)
    place = 0
    for size, p_ref, q_ref in zip(sizes, mine, theirs):
        for i in range(size):
            j, k = place % depth, place // depth
            chip = (own // 2) ^ (j * width + k)
            p, q = p_ref[i], q_ref[i]
            before, after = jnp.where(c == 0, p, q), jnp.where(c == 0, q, p)
            packed[pl.ds(pl.multiple_of(chip * 2 * rows, 2 * rows), 2 * rows), :] = (
                jnp.concatenate([before, after], 0)
            )
            place += 1
    full = lax.dot_general(
        packed[...], downs[...], (((1,), (1,)), ((), ())), preferred_element_type=jnp.float32
    )
    rank = low.shape[1]
    ids = lax.broadcasted_iota(jnp.int32, placement.shape, 1)
    owners = [
        jnp.sum(jnp.where(placement[...] == slot, ids, 0), axis=1, keepdims=True)
        for slot in (own, own ^ 1)
    ]
    adapter = across(index[...])[:, :rank]
    kept = jnp.where(adapter == owners[0], full[:, :rank], 0.0)
    low[...] = jnp.where(adapter == owners[1], full[:, rank:], kept).astype(low.dtype)


def collect(placement, index, downs, mine, theirs, depth, width):
    sizes = [v.shape[0] for v in mine]
    rows, model = mine[0].shape[1:]
    requests = 2 * depth * width * rows
    return pl.pallas_call(
        functools.partial(collect_kernel, depth, width, sizes),
        out_shape=[
            pltpu.VMEM((requests, model), jnp.bfloat16),
            jax.ShapeDtypeStruct((requests, downs.shape[0] // 2), jnp.bfloat16),
        ],
        in_specs=[NEAR] * (3 + 2 * len(sizes)),
        out_specs=[NEAR] * 2,
        cost_estimate=pl.CostEstimate(
            flops=4 * requests * model * 64, bytes_accessed=1 << 20, transcendentals=0
        ),
        compiler_params=pltpu.CompilerParams(vmem_limit_bytes=2 << 20),
        name="collect",
    )(placement, index, near(downs), *[near(v) for v in mine], *[near(v) for v in theirs])


def add_kernel(*refs):
    total = refs[0][...]
    for ref in refs[1:-1]:
        total = total + ref[...]
    refs[-1][...] = total


def add(*values):
    return pl.pallas_call(
        add_kernel,
        out_shape=jax.ShapeDtypeStruct(values[0].shape, values[0].dtype),
        in_specs=[NEAR] * len(values),
        out_specs=NEAR,
        cost_estimate=pl.CostEstimate(flops=0, bytes_accessed=1 << 14, transcendentals=0),
        compiler_params=pltpu.CompilerParams(vmem_limit_bytes=1 << 20),
        name="add",
    )(*values)


def multiply_kernel(start, n, begun, firsts, gating, looped, *refs):
    tokens, refs = refs[1], refs[2:]
    pieces, refs = refs[:n], refs[n:]
    before, refs = refs[:begun], refs[begun:]
    sources, (out, *targets) = refs[: len(firsts)], refs[len(firsts) :]
    copies = copies_of(sources, firsts, targets[:-1], targets[-1]) if firsts else []
    for copy in copies:
        copy.start()

    def tile(here):
        total = piecewise(tokens, pieces, start, here)
        if begun:
            total = total + before[0][:, here]
        out[:, here] = total / (1.0 + jnp.exp(-total)) if gating else total

    if looped:
        for_columns(out.shape[1], tile)
    else:
        for column in range(0, out.shape[1], WIDE):
            tile(pl.ds(column, min(WIDE, out.shape[1] - column)))
    for copy in copies:
        copy.wait()


def multiply(after, tokens, pieces, start, begun, fetched, rows, name, gating=False, looped=True):
    requests = tokens.shape[0]
    hidden = pieces[0].shape[1]
    n = len(fetched)
    operands = [after, near(tokens)] + [near(p) for p in pieces] + [near(b) for b in begun]
    in_specs = [FAR] + [NEAR] * (len(operands) - 1) + [STORED] * n
    operands += [far(source) for source, first in fetched]
    return pl.pallas_call(
        functools.partial(
            multiply_kernel,
            start,
            len(pieces),
            len(begun),
            [first for source, first in fetched],
            gating,
            looped,
        ),
        out_shape=[pltpu.VMEM((requests, hidden), jnp.float32)]
        + [pltpu.VMEM((rows, hidden), tokens.dtype)] * n,
        in_specs=in_specs,
        out_specs=[NEAR] * (1 + n),
        scratch_shapes=[pltpu.SemaphoreType.DMA((n,))] if n else [],
        cost_estimate=pl.CostEstimate(
            flops=2 * requests * sum(p.shape[0] for p in pieces) * hidden,
            bytes_accessed=16 << 20,
            transcendentals=0,
        ),
        compiler_params=pltpu.CompilerParams(vmem_limit_bytes=2 << 20),
        name=name,
    )(*operands)


def finish_kernel(start, n, m, index, tokens, adapter_up, gate, up_pre, *refs):
    pieces, refs = refs[:n], refs[n:]
    lows, (stored, expanded, out, sems) = refs[:m], refs[m:]
    rank = lows[0].shape[1]
    mixed = lows[0][...]
    for low in lows[1:]:
        mixed = mixed + low[...]
    group = TILE // rank
    lane = lax.broadcasted_iota(jnp.int32, (rank, TILE), 1)
    repeat = (lane % rank == lax.broadcasted_iota(jnp.int32, (rank, TILE), 0)).astype(jnp.bfloat16)
    wide = jnp.dot(mixed, repeat, preferred_element_type=jnp.float32)
    of_lane = lax.broadcasted_iota(jnp.int32, (mixed.shape[0], TILE), 1) // rank
    relative = jnp.concatenate([across(index[...])] * (TILE // mixed.shape[0]), 1) - of_lane
    for i in range(expanded.shape[1] // TILE):
        expanded[:, i * TILE : (i + 1) * TILE] = jnp.where(
            relative == i * group, wide, 0.0
        ).astype(jnp.bfloat16)

    width = out.shape[1]
    copies = []
    for first in range(0, width, WIDE):
        here = pl.ds(first, min(WIDE, width - first))
        up = up_pre[:, here] + piecewise(tokens, pieces, start, here)
        up = up + jnp.dot(expanded[...], adapter_up[:, here], preferred_element_type=jnp.float32)
        out[:, here] = (gate[:, here] * up).astype(out.dtype)
        copies.append(
            pltpu.make_async_copy(out.at[:, here], stored.at[:, here], sems.at[len(copies)])
        )
        copies[-1].start()
    for copy in copies:
        copy.wait()


def finish(index, tokens, adapter_up, gate, up_pre, pieces, start, lows):
    requests, hidden = gate.shape
    return pl.pallas_call(
        functools.partial(finish_kernel, start, len(pieces), len(lows)),
        out_shape=jax.ShapeDtypeStruct((requests, hidden), jnp.bfloat16),
        in_specs=[NEAR] * (5 + len(pieces) + len(lows)),
        out_specs=STORED,
        scratch_shapes=[
            pltpu.VMEM((requests, adapter_up.shape[0]), jnp.bfloat16),
            pltpu.VMEM((requests, hidden), jnp.bfloat16),
            pltpu.SemaphoreType.DMA((-(-hidden // WIDE),)),
        ],
        cost_estimate=pl.CostEstimate(
            flops=2 * requests * (adapter_up.shape[0] + sum(p.shape[0] for p in pieces)) * hidden,
            bytes_accessed=4 << 20,
            transcendentals=requests * hidden,
        ),
        compiler_params=pltpu.CompilerParams(vmem_limit_bytes=3 << 20),
        name="finish",
    )(
        index,
        near(tokens),
        near(adapter_up),
        near(gate),
        near(up_pre),
        *[near(p) for p in pieces],
        *lows,
    )


def on_chip(tokens, gate_weight, up_weight, down, up, request_adapter_index, placement):
    depth, width = plan(lax.axis_size("tensor"))
    model, hidden = gate_weight.shape
    index = request_adapter_index[None, :]
    unit = model // PIECES
    firsts = [i * unit for i in range(PIECES)]
    up = up.reshape(-1, hidden)
    down = jnp.swapaxes(down[0], 0, 1)
    own = tokens[None]
    core, column, line_1, line_2 = 1, 2, 2 * width, 4 * width

    block_2 = swap(own, line_2)
    block_1 = swap(own, line_1)
    column_0 = swap(own, column)
    core_down = swap(down, core)
    gates = fetch([(gate_weight, first) for first in firsts[:5]], unit, "fetch_0")
    block_2 = tie(block_2, gates[:1])
    block_3 = swap(block_2, line_1)
    blocks_12 = pack([block_1, block_2], [gates[0], column_0, core_down])
    columns_12 = swap(blocks_12, column)
    *more_gates, downs = fetch(
        [(gate_weight, first) for first in firsts[5:7]],
        unit,
        "fetch_1",
        [blocks_12],
        [down, core_down],
    )
    gates += more_gates
    block_3 = tie(block_3, gates[5:6])
    column_3 = swap(block_3, column)
    line = pack([own, blocks_12, block_3], [])
    core_line = swap(line, core)
    last_gate, *ups = fetch(
        [(gate_weight, firsts[7])] + [(up_weight, first) for first in firsts[:3]],
        unit,
        "fetch_2",
        [line],
    )
    gates.append(last_gate)
    columns = pack([column_0, columns_12, column_3], ups[:1])
    core_columns = swap(columns, core)
    packed, low = collect(
        placement[None, :],
        index,
        downs,
        [line, columns],
        [core_line, core_columns],
        depth,
        width,
    )

    low_1 = add(low, swap(low, line_2))
    gate, *more_ups = multiply(
        low,
        packed,
        gates[:4],
        0,
        [],
        [(up_weight, first) for first in firsts[3:5]],
        unit,
        "gate_a",
    )
    ups += more_ups
    low_2 = add(low_1, swap(low_1, line_1))
    gate, *more_ups = multiply(
        low_1,
        packed,
        gates[4:],
        firsts[4],
        [gate],
        [(up_weight, first) for first in firsts[5:7]],
        unit,
        "gate_b",
        gating=True,
    )
    ups += more_ups
    lows = [low_2, swap(low_2, column)]
    up_pre, last_up = multiply(
        low_2, packed, ups[:5], 0, [], [(up_weight, firsts[7])], unit, "up_a", looped=False
    )
    ups.append(last_up)
    return finish(index, packed, up, gate, up_pre, ups[5:], firsts[5], lows)


def streamed(
    tokens,
    gate_weight,
    up_weight,
    adapter_down_weight,
    adapter_up_weight,
    request_adapter_index,
    adapter_request_lists,
    placement,
):
    count = lax.axis_size("tensor")
    depth, width = plan(count)
    rows = tokens.shape[0]
    requests = request_adapter_index.shape[0]
    adapters = placement.shape[0]
    rank_width = adapter_down_weight.shape[2]
    own = lax.axis_index("tensor")

    by_line = [tokens] + [send(tokens, j, 0, 0) for j in range(1, depth)]
    plane = list(by_line)
    for k in range(1, width):
        plane += [send(block, 0, k, 0) for block in by_line]
    half = jnp.concatenate(plane, 0)
    other = send(half, 0, 0, 1)
    gathered = jnp.concatenate([half, other], 0)

    slot = jnp.arange(requests, dtype=jnp.int32)
    block, inner = slot // rows, slot % rows
    j, k, m = block % depth, block // depth % width, block // (depth * width)
    origin = ((own // (2 * width) - j) % depth * width + (own // 2 - k) % width) * 2 + (own + m) % 2
    row_id = origin * rows + inner

    owner = jnp.sum(jnp.where(placement == own, jnp.arange(adapters, dtype=jnp.int32), 0))
    wanted = lax.dynamic_slice_in_dim(adapter_request_lists, owner, 1, 0)[0]
    picker = (wanted[:, None] == row_id[None, :]).astype(jnp.bfloat16)
    picked = jnp.dot(picker, gathered, preferred_element_type=jnp.float32).astype(jnp.bfloat16)
    low_rank = jnp.dot(picked, adapter_down_weight[0], preferred_element_type=jnp.float32)
    spread = (jnp.arange(requests, dtype=jnp.int32)[:, None] == wanted[None, :]).astype(jnp.bfloat16)
    mixed = jnp.dot(spread, low_rank.astype(jnp.bfloat16), preferred_element_type=jnp.float32)
    mixed = mixed.astype(jnp.bfloat16)
    step = 1
    while step < count:
        mixed = mixed + lax.ppermute(mixed, "tensor", [(i, i ^ step) for i in range(count)])
        step *= 2

    gate_pre = jnp.dot(gathered, gate_weight, preferred_element_type=jnp.float32)
    up_pre = jnp.dot(gathered, up_weight, preferred_element_type=jnp.float32)
    here = (row_id[:, None] == jnp.arange(requests, dtype=jnp.int32)[None, :]).astype(jnp.bfloat16)
    mine = jnp.dot(here, mixed, preferred_element_type=jnp.float32).astype(jnp.bfloat16)
    index = jnp.take(request_adapter_index, row_id)
    chosen = index[:, None] == jnp.arange(adapters, dtype=jnp.int32)[None, :]
    expanded = jnp.where(chosen[:, :, None], mine[:, None, :], jnp.zeros((), jnp.bfloat16))
    delta = jnp.dot(
        expanded.reshape(requests, adapters * rank_width),
        adapter_up_weight.reshape(adapters * rank_width, -1),
        preferred_element_type=jnp.float32,
    )
    hidden = (jax.nn.silu(gate_pre) * (up_pre + delta)).astype(jnp.bfloat16)
    return jnp.dot(here.T, hidden, preferred_element_type=jnp.float32).astype(jnp.bfloat16)


def body(
    tokens,
    gate_weight,
    up_weight,
    adapter_down_weight,
    adapter_up_weight,
    request_adapter_index,
    adapter_request_lists,
    placement,
):
    count = lax.axis_size("tensor")
    if plan(count) == (4, 2) and tokens.shape[0] == 8:
        return on_chip(
            tokens,
            gate_weight,
            up_weight,
            adapter_down_weight,
            adapter_up_weight,
            request_adapter_index,
            placement,
        )
    return streamed(
        tokens,
        gate_weight,
        up_weight,
        adapter_down_weight,
        adapter_up_weight,
        request_adapter_index,
        adapter_request_lists,
        placement,
    )


def solution(mesh):
    in_specs = (
        P(("groups", "tensor"), None),
        P(None, "tensor"),
        P(None, "tensor"),
        P(("groups", "tensor"), None, None),
        P("groups", None, "tensor"),
        P("groups"),
        P("groups", None),
        P("groups"),
    )
    out_specs = P("groups", "tensor")
    return jax.shard_map(body, mesh=mesh, in_specs=in_specs, out_specs=out_specs, check_vma=False)
```
